768 devices in a mesh: pair: 12 (over z_lo, x), grow: 8 (over y), gcol: 8 (over z_hi, core).
Axes of the slice: x: 4, y: 8, z: 12 (z_hi: 4, z_lo: 3; z = z_hi * 3 + z_lo), core: 2. Of those that a mesh axis runs over, the one named last changes fastest.
Arguments:
- valence: bfloat16 [48, 32768], replicated, may hold values from -6 to 6
- conduction: bfloat16 [192, 32768], P('pair'), may hold values from -6 to 6
- valence_energy: float32 [48], replicated, may hold values from -12 to -1
- conduction_energy: float32 [192], P('pair'), may hold values from 0.5 to 8
- pair_valence: int32 [1536], P(('pair', 'grow', 'gcol')), may hold values from 0 to 47
- pair_conduction: int32 [1536], P(('pair', 'grow', 'gcol')), may hold values from 0 to 15
- pair_count: int32 [768], P(('pair', 'grow', 'gcol')), may hold values from 1 to 2, as said below
- g_index: int32 [9216], replicated, may hold values from 1 to 32767, as said below
Outputs:
- chi: float32 [9216, 9216], P(('pair', 'grow'), 'gcol')
The draws below stay inside these ranges and needn't reach their ends.
Inputs may be any that keep to these rules, and one draw needn't show every extreme that they name: `pair_count`: every device has at least one live slot, and some device has exactly 2. `g_index`: distinct cells; with centred frequencies (an index v stands for v - 32 when v >= 16) they are the 9216 cells of smallest |G| other than G = 0 and the planes at frequency -16, closed under G -> -G, in no particular order.
All inputs are finite; a program needn't handle non-finite values.
Results may differ from the reference program's by a relative error of at most 0.0037.
Values may be sent and summed in bfloat16 or wider, within the bound.
No kernel may reach another device: no remote copies, remote signals or barrier semaphores. Data moves between devices by JAX's collectives and lax.ppermute only.
A program may use at most 128 MiB of HBM per device.

```python
import jax
import jax.numpy as jnp
from jax import lax

NV = 48
GRID = 32
NG = 9216
CB_DEV = 16
P_MAX = 2
CB = 192
SLOTS = 1536
GRID3 = 32768
N_GROW = 8
N_GCOL = 8


def draw_pair_count(key, part):
    key = jax.random.fold_in(key, 11)
    first, second = jax.random.split(key)
    devices_total = SLOTS // P_MAX
    counts = jax.random.randint(first, (devices_total,), 1, P_MAX + 1)
    position = jax.random.randint(second, (), 0, devices_total)
    return counts.at[position].set(P_MAX).astype(jnp.int32)


def centred(values):
    return jnp.where(values < GRID // 2, values, values - GRID)


def draw_g_index(key, part):
    key = jax.random.fold_in(key, 23)
    first, second = jax.random.split(key)
    cells = jnp.arange(GRID3, dtype=jnp.int32)
    first_idx = cells // (GRID * GRID)
    second_idx = cells // GRID % GRID
    third_idx = cells % GRID
    partner = ((GRID - first_idx) % GRID * GRID + (GRID - second_idx) % GRID) * GRID + (GRID - third_idx) % GRID
    canonical = jnp.minimum(cells, partner)
    ties = jax.random.permutation(first, GRID3).astype(jnp.int32)[canonical]
    radius = centred(first_idx) ** 2 + centred(second_idx) ** 2 + centred(third_idx) ** 2
    excluded = (first_idx == GRID // 2) | (second_idx == GRID // 2) | (third_idx == GRID // 2) | (cells == 0)
    radius = jnp.where(excluded, 3 * GRID * GRID, radius)
    score = (radius * GRID3 + ties) * 2 + (cells > partner).astype(jnp.int32)
    chosen = jnp.argsort(score, stable=True)[:NG].astype(jnp.int32)
    return jax.random.permutation(second, chosen).astype(jnp.int32)


def place_ends(result, rng, low, largest):
    index_at = [jax.random.randint(jax.random.fold_in(rng, axis), (), 0, length) for axis, length in enumerate(result.shape)]
    main_axis = result.shape.index(max(result.shape))
    next_to = index_at[:main_axis] + [(index_at[main_axis] + 1) % result.shape[main_axis]] + index_at[main_axis + 1:]
    return result.at[tuple(index_at)].set(low).at[tuple(next_to)].set(largest)


def shard_levels(key, shape, cuts, low, high):
    level, own = 1.0, jax.random.fold_in(key, 6)
    for axis_at, shards_of in cuts:
        draws = jnp.exp(jax.random.uniform(jax.random.fold_in(own, axis_at), (shards_of,), jnp.float32, low / len(cuts), high / len(cuts)))
        level = level * jnp.repeat(draws, shape[axis_at] // shards_of).reshape([-1 if axis == axis_at else 1 for axis in range(len(shape))])
    return level


def gaussian(stream_key, extent, width, limit, cuts=(), kind=jnp.bfloat16):
    result = jax.random.normal(stream_key, extent, jnp.float32) * width
    if len(cuts) > 0:
        result = shard_levels(stream_key, extent, cuts, -0.22, 0.18) * result
    return jnp.clip(result, min=-limit, max=limit).astype(kind)


def setup_inputs(seed: int = 0) -> dict:
    key_list = jax.random.split(jax.random.key(seed), 9)
    return {
        "valence": gaussian(key_list[0], (NV, GRID3), 1.0, 6.0),
        "conduction": gaussian(key_list[1], (CB, GRID3), 1.0, 6.0, ((0, 12),)),
        "valence_energy": jnp.clip(jax.random.uniform(key_list[2], (NV,), jnp.float32, -12.0, -1.0), -12.0, -1.0),
        "conduction_energy": jnp.clip(0.5 + 7.5 * jax.random.uniform(key_list[3], (CB,), jnp.float32) ** shard_levels(key_list[3], (CB,), ((0, 12),), -0.2, 0.2), 0.5, 8.0),
        "pair_valence": place_ends(jax.random.randint(key_list[4], (SLOTS,), 0, NV), jax.random.fold_in(key_list[4], 1), 0, NV - 1).astype(jnp.int32),
        "pair_conduction": place_ends(jax.random.randint(key_list[5], (SLOTS,), 0, CB_DEV), jax.random.fold_in(key_list[5], 1), 0, CB_DEV - 1).astype(jnp.int32),
        "pair_count": draw_pair_count(jax.random.fold_in(key_list[8], 71), 0),
        "g_index": draw_g_index(jax.random.fold_in(key_list[8], 71), 0),
    }


def reference(valence, conduction, valence_energy, conduction_energy, pair_valence, pair_conduction, pair_count, g_index):
    slot_ids = jnp.arange(SLOTS, dtype=jnp.int32)
    device_ids = slot_ids // P_MAX
    group_ids = device_ids // (N_GROW * N_GCOL)
    cband = (group_ids * CB_DEV + pair_conduction).astype(jnp.int32)
    live_slots = (slot_ids % P_MAX < pair_count[device_ids]).astype(jnp.float32)
    energy_gap = conduction_energy[cband] - valence_energy[pair_valence]
    factor = live_slots * jnp.sqrt(4.0 / energy_gap) / jnp.sqrt(jnp.float32(GRID3))

    def one_device(inputs):
        vband, cidx, scale = inputs
        density = valence[vband].astype(jnp.float32) * conduction[cidx].astype(jnp.float32)
        spectrum = jnp.fft.fftn(density.reshape(-1, GRID, GRID, GRID), axes=(1, 2, 3)).reshape(-1, GRID3)
        chosen = spectrum[:, g_index]
        real_part = (jnp.real(chosen) * scale[:, None]).astype(jnp.bfloat16)
        imag_part = (jnp.imag(chosen) * scale[:, None]).astype(jnp.bfloat16)
        return (real_part, imag_part)
    blocks = SLOTS // P_MAX
    real_rows, imag_rows = lax.map(one_device, (pair_valence.reshape(blocks, P_MAX), cband.reshape(blocks, P_MAX), factor.reshape(blocks, P_MAX)))
    amplitude = jnp.concatenate([real_rows.reshape(SLOTS, NG), imag_rows.reshape(SLOTS, NG)], axis=0).astype(jnp.float32)
    product = jnp.dot(amplitude.T, amplitude, preferred_element_type=jnp.float32, precision=lax.Precision.HIGHEST)
    return -product / jnp.sqrt(jnp.float32(SLOTS))
```

```python
import numpy as np
import ml_dtypes

import jax
import jax.numpy as jnp
from jax import lax
from jax.experimental import pallas as pl
from jax.experimental.pallas import tpu as pltpu
from jax.sharding import PartitionSpec as P

GRID = 32
NX = 4
LANES = 128
ROWS = 256
CHUNK = 384


def split(table):
    high = table.astype(ml_dtypes.bfloat16)
    low = (table - high.astype(np.float64)).astype(ml_dtypes.bfloat16)
    return high, low


def tables():
    turn = 2.0 * np.pi / GRID
    phase = turn * np.outer(np.arange(32), np.arange(16))
    first = np.concatenate(
        [np.kron(np.eye(4), np.cos(phase)), np.kron(np.eye(4), -np.sin(phase))], axis=1
    )
    high, low = split(first)
    both = np.concatenate([high, low], axis=1)
    lane_table = np.concatenate([both, both], axis=0)
    a_half = np.repeat(np.arange(16), 8)
    beta_half = np.tile(np.arange(8), 16)
    i_row = np.repeat(np.arange(32), 8)
    j_row = np.tile(np.arange(8), 32)
    phase = 2.0 * np.pi * (np.outer(a_half, i_row) / 32.0 + np.outer(beta_half, j_row) / 8.0)
    high, low = split(np.concatenate([np.cos(phase), np.sin(phase)], axis=0))
    row_table = np.concatenate([high, high, low], axis=1)
    beta = np.concatenate([beta_half, (8 - beta_half) % 8])
    angle = turn * np.outer(beta, np.repeat(np.arange(4), 16))
    twiddle_same = np.concatenate([np.cos(angle), np.cos(angle)], axis=1).astype(np.float32)
    twiddle_swap = np.concatenate([np.sin(angle), -np.sin(angle)], axis=1).astype(np.float32)
    step = np.outer(np.arange(4), np.arange(4)) % 4
    real = np.array([1, 0, -1, 0])[step]
    imag = np.array([0, -1, 0, 1])[step]
    last = np.block([[np.kron(real, np.eye(16)), np.kron(imag, np.eye(16))],
                     [np.kron(-imag, np.eye(16)), np.kron(real, np.eye(16))]])
    last_table = np.concatenate([last, last], axis=0).astype(ml_dtypes.bfloat16)
    return lane_table, row_table, twiddle_same, twiddle_swap, last_table


def halves(value):
    high = value.astype(jnp.bfloat16)
    low = (value - high.astype(jnp.float32)).astype(jnp.bfloat16)
    return high, low


def dot(left, right):
    return jnp.dot(left, right, preferred_element_type=jnp.float32)


def select(cells, amplitudes):
    first = cells >> 10
    second = (cells >> 5) & 31
    third = cells & 31
    flip = third >= 16
    first = jnp.where(flip, (32 - first) & 31, first)
    second = jnp.where(flip, (32 - second) & 31, second)
    third = jnp.where(flip, 32 - third, third)
    sign = jnp.where(flip, -1.0, 1.0)
    beta = second & 7
    row = jnp.where(
        first > 16, 128 + (32 - first) * 8 + ((8 - beta) & 7), first * 8 + beta
    )
    lane = (second >> 3) * 16 + third
    width = cells.shape[-1]
    hot = (lax.broadcasted_iota(jnp.int32, (ROWS, width), 0) == row).astype(jnp.bfloat16)
    picked = dot(amplitudes, hot)
    mask = lax.broadcasted_iota(jnp.int32, (64, width), 0) == lane
    parts = []
    for part in range(4):
        block = jnp.where(mask, picked[part * 64:part * 64 + 64], 0.0)
        total = jnp.sum(block, axis=0, keepdims=True)
        parts.append(total * sign if part % 2 else total)
    return jnp.concatenate(parts, axis=0).astype(jnp.bfloat16)


def amplitude_kernel(pv_ref, pc_ref, count_ref, ve_ref, ce_ref, valence_ref, conduction_ref,
                     lane_ref, row_ref, same_ref, swap_ref, last_ref, gcol_ref, grow_ref,
                     col_ref, rowout_ref, bands, wide, amp, sems):
    slots = 2
    copies = []
    for slot in range(slots):
        start = pl.multiple_of(pv_ref[slot] // 16 * 16, 16)
        copies.append(pltpu.make_async_copy(
            valence_ref.at[pl.ds(start, 16), :], bands.at[slot], sems.at[slot]))
    copies.append(pltpu.make_async_copy(conduction_ref, bands.at[slots], sems.at[slots]))
    for copy in copies:
        copy.start()
    for copy in copies:
        copy.wait()

    def widen(tile, carry):
        lanes = pl.ds(pl.multiple_of(tile * LANES, LANES), LANES)
        rows = pl.ds(pl.multiple_of(tile * 16, 16), 16)
        for band in range(slots + 1):
            wide[band, rows, :] = bands[band, :, lanes].astype(jnp.float32)
        return carry

    lax.fori_loop(0, ROWS, widen, 0, unroll=8)

    stage = []
    for slot in range(slots):
        left = wide[slot, pl.ds(pv_ref[slot] % 16, ROWS, stride=16), :]
        right = wide[slots, pl.ds(pc_ref[slot], ROWS, stride=16), :]
        high, low = halves(left * right)
        out = dot(jnp.concatenate([high, low], axis=1), lane_ref[...])
        stage.append(out[:, :LANES] + out[:, LANES:])
    high, low = halves(jnp.concatenate(stage, axis=1))
    out = dot(row_ref[...], jnp.concatenate([high, low, high], axis=0))
    lane_id = lax.broadcasted_iota(jnp.int32, (LANES, LANES), 1)
    for slot in range(slots):
        lanes = slice(slot * LANES, slot * LANES + LANES)
        cosine, sine = out[:LANES, lanes], out[LANES:, lanes]
        turned = pltpu.roll(sine, 64, 1)
        turned = jnp.where(lane_id < 64, turned, -turned)
        full = jnp.concatenate([cosine + turned, cosine - turned], axis=0)
        full = full * same_ref[...] + pltpu.roll(full, 64, 1) * swap_ref[...]
        high, low = halves(full)
        spectrum = dot(jnp.concatenate([high, low], axis=1), last_ref[...])
        gap = ce_ref[pc_ref[slot]] - ve_ref[pv_ref[slot]]
        live = jnp.where(slot < count_ref[0], 1.0, 0.0)
        factor = live * jnp.sqrt(4.0 / jnp.full((1, LANES), gap, jnp.float32)) / np.float32(
            np.sqrt(np.float32(GRID**3)))
        amp[slot * LANES:slot * LANES + LANES, :] = (spectrum * factor).T.astype(jnp.bfloat16)

    parts = col_ref.shape[2] // CHUNK

    def pick_columns(block, carry):
        for part in range(parts):
            cells = gcol_ref[pl.ds(block * parts + part, 1), :]
            col_ref[block, :, part * CHUNK:part * CHUNK + CHUNK] = select(cells, amp[...])
        return carry

    def pick_rows(block, carry):
        picked = select(grow_ref[pl.ds(block, 1), :], amp[...])
        rowout_ref[block] = picked[:, :rowout_ref.shape[2]]
        return carry

    lax.fori_loop(0, rowout_ref.shape[0], pick_rows, 0)
    lax.fori_loop(0, col_ref.shape[0], pick_columns, 0)


def amplitudes_of(pv, pc, count, ve, ce, valence, conduction, gcol, grow, col_shape, row_shape):
    smem = pl.BlockSpec(memory_space=pltpu.SMEM)
    vmem = pl.BlockSpec(memory_space=pltpu.VMEM)
    hbm = pl.BlockSpec(memory_space=pl.ANY)
    return pl.pallas_call(
        amplitude_kernel,
        out_shape=(jax.ShapeDtypeStruct(col_shape, jnp.bfloat16),
                   jax.ShapeDtypeStruct(row_shape, jnp.bfloat16)),
        in_specs=[smem] * 5 + [hbm] * 2 + [vmem] * 7,
        out_specs=(vmem, vmem),
        scratch_shapes=[
            pltpu.VMEM((3, 16, GRID**3), jnp.bfloat16),
            pltpu.VMEM((3, 16 * ROWS, LANES), jnp.float32),
            pltpu.VMEM((ROWS, ROWS), jnp.bfloat16),
            pltpu.SemaphoreType.DMA((3,)),
        ],
        compiler_params=pltpu.CompilerParams(vmem_limit_bytes=40 * 1024 * 1024),
        cost_estimate=pl.CostEstimate(flops=4 * 10**9, bytes_accessed=5 * 10**6, transcendentals=0),
    )(pv, pc, count, ve, ce, valence, conduction, *(jnp.asarray(t) for t in tables()), gcol, grow)


def local(valence, conduction, valence_energy, conduction_energy, pair_valence, pair_conduction,
          pair_count, g_index):
    n_pair, n_grow, n_gcol = (lax.axis_size(name) for name in ("pair", "grow", "gcol"))
    n_z = n_pair // NX
    total_g = g_index.shape[0]
    doubled = 2 * pair_valence.shape[0]
    width = total_g // n_gcol
    sub = total_g // (n_pair * n_grow)
    n_xy = NX * n_grow
    x_groups = [[z * NX + x for x in range(NX)] for z in range(n_z)]
    z_groups = [[z * NX + x for z in range(n_z)] for x in range(NX)]
    xy_groups = [[(z * NX + x) * n_grow + y for x in range(NX) for y in range(n_grow)]
                 for z in range(n_z)]
    g_rows = g_index.reshape(n_z, n_xy, sub).transpose(1, 0, 2).reshape(n_xy, n_z * sub)
    g_rows = jnp.pad(g_rows, ((0, 0), (0, CHUNK - n_z * sub)))
    col, row = amplitudes_of(
        pair_valence, pair_conduction, pair_count, valence_energy, conduction_energy,
        valence, conduction, g_index.reshape(total_g // CHUNK, CHUNK), g_rows,
        (n_gcol, doubled, width), (n_xy, doubled, n_z * sub))
    row = lax.all_to_all(row, ("pair", "grow"), 0, 0, tiled=True, axis_index_groups=xy_groups)
    col = lax.all_to_all(col, "gcol", 0, 0, tiled=True)
    row = lax.all_gather(row.reshape(1, n_xy * doubled, n_z * sub), "gcol", axis=0, tiled=True)
    col = lax.all_gather(col.reshape(1, n_gcol * doubled, width), "grow", axis=0, tiled=True)
    col = lax.all_gather(col, "pair", axis=0, tiled=True, axis_index_groups=x_groups)
    row = row.reshape(n_gcol, n_xy, doubled, n_z * sub).transpose(1, 0, 2, 3)
    row = row.reshape(-1, n_z * sub)
    col = col.reshape(-1, width)
    partial = lax.dot_general(row, col, (((0,), (0,)), ((), ())),
                              preferred_element_type=jnp.float32)
    partial = partial.astype(jnp.bfloat16).reshape(n_z, sub, width)
    partial = lax.all_to_all(partial, "pair", 0, 0, tiled=True, axis_index_groups=z_groups)
    summed = jnp.sum(partial.astype(jnp.float32), axis=0)
    total_slots = pair_valence.shape[0] * n_pair * n_grow * n_gcol
    return -summed / jnp.sqrt(jnp.float32(total_slots))


def solution(mesh):
    return jax.shard_map(
        local,
        mesh=mesh,
        in_specs=(
            P(),
            P("pair", None),
            P(),
            P("pair"),
            P(("pair", "grow", "gcol")),
            P(("pair", "grow", "gcol")),
            P(("pair", "grow", "gcol")),
            P(),
        ),
        out_specs=P(("pair", "grow"), "gcol"),
        check_vma=False,
    )
```

```python
import numpy as np
import ml_dtypes

import jax
import jax.numpy as jnp
from jax import lax
from jax.experimental import pallas as pl
from jax.experimental.pallas import tpu as pltpu
from jax.sharding import PartitionSpec as P

GRID = 32
NX = 4
LANES = 128
ROWS = 256
CHUNK = 384


def split(table):
    high = table.astype(ml_dtypes.bfloat16)
    low = (table - high.astype(np.float64)).astype(ml_dtypes.bfloat16)
    return high, low


def tables():
    turn = 2.0 * np.pi / GRID
    phase = turn * np.outer(np.arange(32), np.arange(16))
    first = np.concatenate(
        [np.kron(np.eye(4), np.cos(phase)), np.kron(np.eye(4), -np.sin(phase))], axis=1
    )
    high, low = split(first)
    both = np.concatenate([high, low], axis=1)
    lane_table = np.concatenate([both, both], axis=0)
    a_half = np.repeat(np.arange(16), 8)
    beta_half = np.tile(np.arange(8), 16)
    i_row = np.repeat(np.arange(32), 8)
    j_row = np.tile(np.arange(8), 32)
    phase = 2.0 * np.pi * (np.outer(a_half, i_row) / 32.0 + np.outer(beta_half, j_row) / 8.0)
    high, low = split(np.concatenate([np.cos(phase), np.sin(phase)], axis=0))
    row_table = np.concatenate([high, high, low], axis=1)
    beta = np.concatenate([beta_half, (8 - beta_half) % 8])
    angle = turn * np.outer(beta, np.repeat(np.arange(4), 16))
    twiddle_same = np.concatenate([np.cos(angle), np.cos(angle)], axis=1).astype(np.float32)
    twiddle_swap = np.concatenate([np.sin(angle), -np.sin(angle)], axis=1).astype(np.float32)
    step = np.outer(np.arange(4), np.arange(4)) % 4
    real = np.array([1, 0, -1, 0])[step]
    imag = np.array([0, -1, 0, 1])[step]
    last = np.block([[np.kron(real, np.eye(16)), np.kron(imag, np.eye(16))],
                     [np.kron(-imag, np.eye(16)), np.kron(real, np.eye(16))]])
    last_table = np.concatenate([last, last], axis=0).astype(ml_dtypes.bfloat16)
    return lane_table, row_table, twiddle_same, twiddle_swap, last_table


def halves(value):
    high = value.astype(jnp.bfloat16)
    low = (value - high.astype(jnp.float32)).astype(jnp.bfloat16)
    return high, low


def dot(left, right):
    return jnp.dot(left, right, preferred_element_type=jnp.float32)


def select(cells, amplitudes):
    first = cells >> 10
    second = (cells >> 5) & 31
    third = cells & 31
    flip = third >= 16
    first = jnp.where(flip, (32 - first) & 31, first)
    second = jnp.where(flip, (32 - second) & 31, second)
    third = jnp.where(flip, 32 - third, third)
    sign = jnp.where(flip, -1.0, 1.0)
    beta = second & 7
    row = jnp.where(
        first > 16, 128 + (32 - first) * 8 + ((8 - beta) & 7), first * 8 + beta
    )
    lane = (second >> 3) * 16 + third
    width = cells.shape[-1]
    hot = (lax.broadcasted_iota(jnp.int32, (ROWS, width), 0) == row).astype(jnp.bfloat16)
    picked = dot(amplitudes, hot)
    mask = lax.broadcasted_iota(jnp.int32, (64, width), 0) == lane
    parts = []
    for part in range(4):
        block = jnp.where(mask, picked[part * 64:part * 64 + 64], 0.0)
        total = jnp.sum(block, axis=0, keepdims=True)
        parts.append(total * sign if part % 2 else total)
    return jnp.concatenate(parts, axis=0)


def lane_tiles(width):
    return [(lane, min(LANES, width - lane)) for lane in range(0, width, LANES)]


def amplitude_kernel(pv_hbm, pc_hbm, count_hbm, ve_hbm, ce_hbm, valence_hbm, conduction_hbm,
                     lane_hbm, row_hbm, same_hbm, swap_hbm, last_hbm, g_hbm,
                     out_ref, pv_ref, pc_ref, count_ref, ve_ref, ce_ref, valence_ref,
                     conduction_ref, lane_ref, row_ref, same_ref, swap_ref, last_ref, g_ref,
                     wide, amp, flat, ordered, sems):
    slots = 2
    sub = out_ref.shape[2] // 3
    n_xy = out_ref.shape[1] // (2 * slots)
    sources = (pv_hbm, pc_hbm, conduction_hbm, valence_hbm, lane_hbm, row_hbm, same_hbm,
               swap_hbm, last_hbm, g_hbm, count_hbm, ve_hbm, ce_hbm)
    targets = (pv_ref, pc_ref, conduction_ref, valence_ref, lane_ref, row_ref, same_ref,
               swap_ref, last_ref, g_ref, count_ref, ve_ref, ce_ref)
    copies = [pltpu.make_async_copy(source, target, sems.at[at])
              for at, (source, target) in enumerate(zip(sources, targets))]
    for copy in copies:
        copy.start()
    for copy in copies[:4]:
        copy.wait()
    picks = [(valence_ref, pv_ref[slot]) for slot in range(slots)]
    picks += [(conduction_ref, pc_ref[slot]) for slot in range(slots)]

    def widen(tile, carry):
        lanes = pl.ds(pl.multiple_of(tile * LANES, LANES), LANES)
        rows = pl.ds(pl.multiple_of(tile * 8, 8), 8)
        for at, (ref, band) in enumerate(picks):
            start = pl.multiple_of(band // 16 * 16, 16)
            block = ref[pl.ds(start, 16), lanes].astype(jnp.float32)
            wide[at, rows, :] = jnp.where(band % 16 >= 8, block[8:], block[:8])
        return carry

    lax.fori_loop(0, ROWS, widen, 0, unroll=8)
    for copy in copies[4:]:
        copy.wait()

    stage = []
    for slot in range(slots):
        left = wide[slot, pl.ds(pv_ref[slot] % 8, ROWS, stride=8), :]
        right = wide[slots + slot, pl.ds(pc_ref[slot] % 8, ROWS, stride=8), :]
        high, low = halves(left * right)
        out = dot(jnp.concatenate([high, low], axis=1), lane_ref[...])
        stage.append(out[:, :LANES] + out[:, LANES:])
    high, low = halves(jnp.concatenate(stage, axis=1))
    out = dot(row_ref[...], jnp.concatenate([high, low, high], axis=0))
    lane_id = lax.broadcasted_iota(jnp.int32, (LANES, LANES), 1)
    for slot in range(slots):
        lanes = slice(slot * LANES, slot * LANES + LANES)
        cosine, sine = out[:LANES, lanes], out[LANES:, lanes]
        turned = pltpu.roll(sine, 64, 1)
        turned = jnp.where(lane_id < 64, turned, -turned)
        full = jnp.concatenate([cosine + turned, cosine - turned], axis=0)
        full = full * same_ref[...] + pltpu.roll(full, 64, 1) * swap_ref[...]
        high, low = halves(full)
        spectrum = dot(jnp.concatenate([high, low], axis=1), last_ref[...])
        gap = ce_ref[pc_ref[slot]] - ve_ref[pv_ref[slot]]
        live = jnp.where(slot < count_ref[0], 1.0, 0.0)
        factor = live * jnp.sqrt(4.0 / jnp.full((1, LANES), gap, jnp.float32)) / np.float32(
            np.sqrt(np.float32(GRID**3)))
        amp[slot * LANES:slot * LANES + LANES, :] = (spectrum * factor).T.astype(jnp.bfloat16)

    per = CHUNK // LANES

    def pick(chunk, carry):
        cells = jnp.concatenate(
            [g_ref[pl.ds(chunk * per + at, 1), :] for at in range(per)], axis=1)
        lanes = pl.ds(pl.multiple_of(chunk * CHUNK, CHUNK), CHUNK)
        flat[0:4, lanes] = select(cells, amp[...])
        return carry

    lax.fori_loop(0, flat.shape[1] // CHUNK, pick, 0, unroll=3)
    for place in range(n_xy):
        starts = [(z * n_xy + place) * sub for z in range(3)]
        block = jnp.concatenate([flat[0:4, at:at + sub] for at in starts], axis=1)
        for at, (lane, size) in enumerate(lane_tiles(3 * sub)):
            part = block[:, lane:lane + size]
            if size < LANES:
                part = jnp.concatenate(
                    [part, jnp.zeros((4, LANES - size), jnp.float32)], axis=1)
            ordered[at, pl.ds(place, 4, stride=n_xy), :] = part
    for at, (lane, size) in enumerate(lane_tiles(3 * sub)):
        out_ref[0, :, lane:lane + size] = ordered[at, :, :size].astype(jnp.bfloat16)


def amplitudes_of(pv, pc, count, ve, ce, valence, conduction, g_index, n_xy, wide_sub):
    hbm = pl.BlockSpec(memory_space=pltpu.HBM)
    consts = [jnp.asarray(table) for table in tables()]
    g_rows = g_index.reshape(-1, LANES)
    arrays = [valence, conduction, *consts, g_rows]
    doubled = 2 * pv.shape[0]
    return pl.pallas_call(
        amplitude_kernel,
        out_shape=jax.ShapeDtypeStruct((1, doubled * n_xy, wide_sub), jnp.bfloat16),
        in_specs=[hbm] * 13,
        out_specs=pl.BlockSpec(memory_space=pltpu.VMEM),
        scratch_shapes=[pltpu.SMEM(a.shape, a.dtype) for a in (pv, pc, count, ve, ce)]
        + [pltpu.VMEM(a.shape, a.dtype) for a in arrays]
        + [
            pltpu.VMEM((4, 8 * ROWS, LANES), jnp.float32),
            pltpu.VMEM((ROWS, ROWS), jnp.bfloat16),
            pltpu.VMEM((8, g_index.shape[0]), jnp.float32),
            pltpu.VMEM((-(-wide_sub // LANES), doubled * n_xy, LANES), jnp.float32),
            pltpu.SemaphoreType.DMA((13,)),
        ],
        compiler_params=pltpu.CompilerParams(vmem_limit_bytes=40 * 1024 * 1024),
        cost_estimate=pl.CostEstimate(flops=4 * 10**9, bytes_accessed=5 * 10**6, transcendentals=0),
    )(pv, pc, count, ve, ce, *arrays)


def deal_kernel(mine_ref, all_ref, rows_ref, col_ref, wide):
    n_xy, depth, wide_sub = rows_ref.shape
    sub = wide_sub // 3
    blocks = col_ref.shape[1] // depth * 3
    tiles = lane_tiles(wide_sub)
    for at, (lane, size) in enumerate(tiles):
        block = all_ref[:, :, lane:lane + size].astype(jnp.float32)
        wide[at, :, :size] = block.reshape(n_xy * depth, size)
    for place in range(n_xy):
        for at, (lane, size) in enumerate(tiles):
            rows = wide[at, pl.ds(place, depth, stride=n_xy), :]
            rows_ref[place, :, lane:lane + size] = rows[:, :size].astype(jnp.bfloat16)
    for chunk in range(blocks // 3):
        parts = []
        for at in range(3):
            block = mine_ref[0] * blocks + chunk * 3 + at
            layer, place = block // n_xy, block % n_xy
            rows = jnp.concatenate(
                [wide[tile, pl.ds(place, depth, stride=n_xy), :] for tile in range(len(tiles))],
                axis=1)[:, :wide_sub]
            part = jnp.where(layer == 1, rows[:, sub:2 * sub], rows[:, :sub])
            parts.append(jnp.where(layer == 2, rows[:, 2 * sub:], part))
        col_ref[0, chunk * depth:chunk * depth + depth, :] = jnp.concatenate(
            parts, axis=1).astype(jnp.bfloat16)


def deal(mine, gathered, n_xy, width):
    n_gcol, rows, wide_sub = gathered.shape
    depth = n_gcol * rows // n_xy
    vmem = pl.BlockSpec(memory_space=pltpu.VMEM)
    return pl.pallas_call(
        deal_kernel,
        out_shape=(jax.ShapeDtypeStruct((n_xy, depth, wide_sub), jnp.bfloat16),
                   jax.ShapeDtypeStruct((1, width // wide_sub * depth, wide_sub), jnp.bfloat16)),
        in_specs=[pl.BlockSpec(memory_space=pltpu.SMEM), vmem],
        out_specs=(vmem, vmem),
        scratch_shapes=[pltpu.VMEM((-(-wide_sub // LANES), n_gcol * rows, LANES), jnp.float32)],
        compiler_params=pltpu.CompilerParams(vmem_limit_bytes=16 * 1024 * 1024),
        cost_estimate=pl.CostEstimate(flops=10**6, bytes_accessed=2 * 10**6, transcendentals=0),
    )(mine, gathered)


def tile_kernel(row_ref, col_ref, out_ref):
    n_xy, depth, wide_sub = row_ref.shape
    left = row_ref[...].reshape(n_xy * depth, wide_sub)
    parts = []
    for chunk in range(col_ref.shape[1] // depth):
        right = col_ref[:, chunk * depth:chunk * depth + depth, :]
        parts.append(lax.dot_general(
            left, right.reshape(n_xy * depth, wide_sub), (((0,), (0,)), ((), ())),
            preferred_element_type=jnp.float32))
    out_ref[...] = jnp.concatenate(parts, axis=1).astype(jnp.bfloat16)


def tile(row, col):
    n_xy, depth, wide_sub = row.shape
    width = col.shape[1] // depth * wide_sub
    vmem = pl.BlockSpec(memory_space=pltpu.VMEM)
    return pl.pallas_call(
        tile_kernel,
        out_shape=jax.ShapeDtypeStruct((wide_sub, width), jnp.bfloat16),
        in_specs=[vmem, vmem],
        out_specs=vmem,
        compiler_params=pltpu.CompilerParams(vmem_limit_bytes=40 * 1024 * 1024),
        cost_estimate=pl.CostEstimate(
            flops=2 * n_xy * depth * wide_sub * width, bytes_accessed=5 * 10**6, transcendentals=0),
    )(row, col)


def local(valence, conduction, valence_energy, conduction_energy, pair_valence, pair_conduction,
          pair_count, g_index):
    n_pair, n_grow, n_gcol = (lax.axis_size(name) for name in ("pair", "grow", "gcol"))
    n_z = n_pair // NX
    total_g = g_index.shape[0]
    width = total_g // n_gcol
    sub = total_g // (n_pair * n_grow)
    n_xy = NX * n_grow
    x_groups = [[z * NX + x for x in range(NX)] for z in range(n_z)]
    z_groups = [[z * NX + x for z in range(n_z)] for x in range(NX)]
    xy_groups = [[(z * NX + x) * n_grow + y for x in range(NX) for y in range(n_grow)]
                 for z in range(n_z)]
    mine = amplitudes_of(
        pair_valence, pair_conduction, pair_count, valence_energy, conduction_energy,
        valence, conduction, g_index, n_xy, n_z * sub)
    mine = lax.all_gather(mine, "gcol", axis=0, tiled=True)
    row, col = deal(lax.axis_index("gcol").astype(jnp.int32)[None], mine, n_xy, width)
    row = lax.all_to_all(row, ("pair", "grow"), 0, 0, tiled=True, axis_index_groups=xy_groups)
    col = lax.all_gather(col, "grow", axis=0, tiled=True)
    col = lax.all_gather(col, "pair", axis=0, tiled=True, axis_index_groups=x_groups)
    partial = tile(row, col).reshape(n_z, sub, width)
    partial = lax.all_to_all(partial, "pair", 0, 0, tiled=True, axis_index_groups=z_groups)
    summed = jnp.sum(partial.astype(jnp.float32), axis=0)
    total_slots = pair_valence.shape[0] * n_pair * n_grow * n_gcol
    return -summed / jnp.sqrt(jnp.float32(total_slots))


def solution(mesh):
    return jax.shard_map(
        local,
        mesh=mesh,
        in_specs=(
            P(),
            P("pair", None),
            P(),
            P("pair"),
            P(("pair", "grow", "gcol")),
            P(("pair", "grow", "gcol")),
            P(("pair", "grow", "gcol")),
            P(),
        ),
        out_specs=P(("pair", "grow"), "gcol"),
        check_vma=False,
    )
```

```python
import numpy as np
import ml_dtypes

import jax
import jax.numpy as jnp
from jax import lax
from jax.experimental import pallas as pl
from jax.experimental.pallas import tpu as pltpu
from jax.sharding import PartitionSpec as P

GRID = 32
NX = 4
LANES = 128
ROWS = 256
CHUNK = 384


def split(table):
    high = table.astype(ml_dtypes.bfloat16)
    low = (table - high.astype(np.float64)).astype(ml_dtypes.bfloat16)
    return high, low


def tables():
    turn = 2.0 * np.pi / GRID
    phase = turn * np.outer(np.arange(32), np.arange(16))
    first = np.concatenate(
        [np.kron(np.eye(4), np.cos(phase)), np.kron(np.eye(4), -np.sin(phase))], axis=1
    )
    high, low = split(first)
    both = np.concatenate([high, low], axis=1)
    lane_table = np.concatenate([both, both], axis=0)
    a_half = np.repeat(np.arange(16), 8)
    beta_half = np.tile(np.arange(8), 16)
    i_row = np.repeat(np.arange(32), 8)
    j_row = np.tile(np.arange(8), 32)
    phase = 2.0 * np.pi * (np.outer(a_half, i_row) / 32.0 + np.outer(beta_half, j_row) / 8.0)
    high, low = split(np.concatenate([np.cos(phase), np.sin(phase)], axis=0))
    row_table = np.concatenate([high, high, low], axis=1)
    beta = np.concatenate([beta_half, (8 - beta_half) % 8])
    angle = turn * np.outer(beta, np.repeat(np.arange(4), 16))
    twiddle_same = np.concatenate([np.cos(angle), np.cos(angle)], axis=1).astype(np.float32)
    twiddle_swap = np.concatenate([np.sin(angle), -np.sin(angle)], axis=1).astype(np.float32)
    step = np.outer(np.arange(4), np.arange(4)) % 4
    real = np.array([1, 0, -1, 0])[step]
    imag = np.array([0, -1, 0, 1])[step]
    last = np.block([[np.kron(real, np.eye(16)), np.kron(imag, np.eye(16))],
                     [np.kron(-imag, np.eye(16)), np.kron(real, np.eye(16))]])
    last_table = np.concatenate([last, last], axis=0).astype(ml_dtypes.bfloat16)
    return lane_table, row_table, twiddle_same, twiddle_swap, last_table


def halves(value):
    high = value.astype(jnp.bfloat16)
    low = (value - high.astype(jnp.float32)).astype(jnp.bfloat16)
    return high, low


def position(name):
    return lax.axis_index(name)


def dot(left, right):
    return jnp.dot(left, right, preferred_element_type=jnp.float32)


def select(cells, amplitudes):
    first = cells >> 10
    second = (cells >> 5) & 31
    third = cells & 31
    flip = third >= 16
    first = jnp.where(flip, (32 - first) & 31, first)
    second = jnp.where(flip, (32 - second) & 31, second)
    third = jnp.where(flip, 32 - third, third)
    sign = jnp.where(flip, -1.0, 1.0)
    beta = second & 7
    row = jnp.where(
        first > 16, 128 + (32 - first) * 8 + ((8 - beta) & 7), first * 8 + beta
    )
    lane = (second >> 3) * 16 + third
    width = cells.shape[-1]
    hot = (lax.broadcasted_iota(jnp.int32, (ROWS, width), 0) == row).astype(jnp.bfloat16)
    picked = dot(amplitudes, hot)
    mask = lax.broadcasted_iota(jnp.int32, (64, width), 0) == lane
    parts = []
    for part in range(4):
        block = jnp.where(mask, picked[part * 64:part * 64 + 64], 0.0)
        total = jnp.sum(block, axis=0, keepdims=True)
        parts.append(total * sign if part % 2 else total)
    return jnp.concatenate(parts, axis=0)


def lane_tiles(width):
    return [(lane, min(LANES, width - lane)) for lane in range(0, width, LANES)]


def amplitude_kernel(pv_hbm, pc_hbm, count_hbm, ve_hbm, ce_hbm, valence_hbm, conduction_hbm,
                     lane_hbm, row_hbm, same_hbm, swap_hbm, last_hbm, g_hbm,
                     out_ref, pv_ref, pc_ref, count_ref, ve_ref, ce_ref, valence_ref,
                     conduction_ref, lane_ref, row_ref, same_ref, swap_ref, last_ref, g_ref,
                     wide, amp, flat, ordered, sems):
    slots = 2
    sub = out_ref.shape[2] // 3
    n_xy = out_ref.shape[1] // (2 * slots)
    sources = (pv_hbm, pc_hbm, conduction_hbm, valence_hbm, lane_hbm, row_hbm, same_hbm,
               swap_hbm, last_hbm, g_hbm, count_hbm, ve_hbm, ce_hbm)
    targets = (pv_ref, pc_ref, conduction_ref, valence_ref, lane_ref, row_ref, same_ref,
               swap_ref, last_ref, g_ref, count_ref, ve_ref, ce_ref)
    copies = [pltpu.make_async_copy(source, target, sems.at[at])
              for at, (source, target) in enumerate(zip(sources, targets))]
    for copy in copies:
        copy.start()
    for copy in copies[:4]:
        copy.wait()
    picks = [(valence_ref, pv_ref[slot]) for slot in range(slots)]
    picks += [(conduction_ref, pc_ref[slot]) for slot in range(slots)]

    def widen(tile, carry):
        lanes = pl.ds(pl.multiple_of(tile * LANES, LANES), LANES)
        rows = pl.ds(pl.multiple_of(tile * 8, 8), 8)
        for at, (ref, band) in enumerate(picks):
            start = pl.multiple_of(band // 16 * 16, 16)
            block = ref[pl.ds(start, 16), lanes].astype(jnp.float32)
            wide[at, rows, :] = jnp.where(band % 16 >= 8, block[8:], block[:8])
        return carry

    lax.fori_loop(0, ROWS, widen, 0, unroll=8)
    for copy in copies[4:]:
        copy.wait()

    stage = []
    for slot in range(slots):
        left = wide[slot, pl.ds(pv_ref[slot] % 8, ROWS, stride=8), :]
        right = wide[slots + slot, pl.ds(pc_ref[slot] % 8, ROWS, stride=8), :]
        high, low = halves(left * right)
        out = dot(jnp.concatenate([high, low], axis=1), lane_ref[...])
        stage.append(out[:, :LANES] + out[:, LANES:])
    high, low = halves(jnp.concatenate(stage, axis=1))
    out = dot(row_ref[...], jnp.concatenate([high, low, high], axis=0))
    lane_id = lax.broadcasted_iota(jnp.int32, (LANES, LANES), 1)
    for slot in range(slots):
        lanes = slice(slot * LANES, slot * LANES + LANES)
        cosine, sine = out[:LANES, lanes], out[LANES:, lanes]
        turned = pltpu.roll(sine, 64, 1)
        turned = jnp.where(lane_id < 64, turned, -turned)
        full = jnp.concatenate([cosine + turned, cosine - turned], axis=0)
        full = full * same_ref[...] + pltpu.roll(full, 64, 1) * swap_ref[...]
        high, low = halves(full)
        spectrum = dot(jnp.concatenate([high, low], axis=1), last_ref[...])
        gap = ce_ref[pc_ref[slot]] - ve_ref[pv_ref[slot]]
        live = jnp.where(slot < count_ref[0], 1.0, 0.0)
        factor = live * jnp.sqrt(4.0 / jnp.full((1, LANES), gap, jnp.float32)) / np.float32(
            np.sqrt(np.float32(GRID**3)))
        amp[slot * LANES:slot * LANES + LANES, :] = (spectrum * factor).T.astype(jnp.bfloat16)

    per = CHUNK // LANES

    def pick(chunk, carry):
        cells = jnp.concatenate(
            [g_ref[pl.ds(chunk * per + at, 1), :] for at in range(per)], axis=1)
        lanes = pl.ds(pl.multiple_of(chunk * CHUNK, CHUNK), CHUNK)
        flat[0:4, lanes] = select(cells, amp[...])
        return carry

    lax.fori_loop(0, flat.shape[1] // CHUNK, pick, 0, unroll=3)
    for place in range(n_xy):
        starts = [(z * n_xy + place) * sub for z in range(3)]
        block = jnp.concatenate([flat[0:4, at:at + sub] for at in starts], axis=1)
        for at, (lane, size) in enumerate(lane_tiles(3 * sub)):
            part = block[:, lane:lane + size]
            if size < LANES:
                part = jnp.concatenate(
                    [part, jnp.zeros((4, LANES - size), jnp.float32)], axis=1)
            ordered[at, pl.ds(place, 4, stride=n_xy), :] = part
    for at, (lane, size) in enumerate(lane_tiles(3 * sub)):
        out_ref[0, :, lane:lane + size] = ordered[at, :, :size].astype(jnp.bfloat16)


def amplitudes_of(pv, pc, count, ve, ce, valence, conduction, g_index, n_xy, wide_sub):
    hbm = pl.BlockSpec(memory_space=pltpu.HBM)
    consts = [jnp.asarray(table) for table in tables()]
    g_rows = g_index.reshape(-1, LANES)
    arrays = [valence, conduction, *consts, g_rows]
    doubled = 2 * pv.shape[0]
    return pl.pallas_call(
        amplitude_kernel,
        out_shape=jax.ShapeDtypeStruct((1, doubled * n_xy, wide_sub), jnp.bfloat16),
        in_specs=[hbm] * 13,
        out_specs=pl.BlockSpec(memory_space=pltpu.VMEM),
        scratch_shapes=[pltpu.SMEM(a.shape, a.dtype) for a in (pv, pc, count, ve, ce)]
        + [pltpu.VMEM(a.shape, a.dtype) for a in arrays]
        + [
            pltpu.VMEM((4, 8 * ROWS, LANES), jnp.float32),
            pltpu.VMEM((ROWS, ROWS), jnp.bfloat16),
            pltpu.VMEM((8, g_index.shape[0]), jnp.float32),
            pltpu.VMEM((-(-wide_sub // LANES), doubled * n_xy, LANES), jnp.float32),
            pltpu.SemaphoreType.DMA((13,)),
        ],
        compiler_params=pltpu.CompilerParams(vmem_limit_bytes=60 * 1024 * 1024),
        cost_estimate=pl.CostEstimate(flops=4 * 10**9, bytes_accessed=5 * 10**6, transcendentals=0),
    )(pv, pc, count, ve, ce, *arrays)


def deal_kernel(all_ref, rows_ref, col_ref, wide):
    n_xy, depth, wide_sub = rows_ref.shape
    sub = wide_sub // 3
    blocks = col_ref.shape[2] // sub
    tiles = lane_tiles(wide_sub)
    for at, (lane, size) in enumerate(tiles):
        block = all_ref[:, :, lane:lane + size].astype(jnp.float32)
        wide[at, :, :size] = block.reshape(n_xy * depth, size)
    for place in range(n_xy):
        for at, (lane, size) in enumerate(tiles):
            rows = wide[at, pl.ds(place, depth, stride=n_xy), :]
            rows_ref[place, :, lane:lane + size] = rows[:, :size].astype(jnp.bfloat16)
    mine = position("gcol") * blocks
    parts = []
    for at in range(blocks):
        layer, place = (mine + at) // n_xy, (mine + at) % n_xy
        rows = jnp.concatenate(
            [wide[tile, pl.ds(place, depth, stride=n_xy), :] for tile in range(len(tiles))],
            axis=1)[:, :wide_sub]
        part = jnp.where(layer == 1, rows[:, sub:2 * sub], rows[:, :sub])
        parts.append(jnp.where(layer == 2, rows[:, 2 * sub:], part))
    whole = jnp.concatenate(parts, axis=1).astype(jnp.bfloat16)
    for target in range(col_ref.shape[0]):
        col_ref[target] = whole


def deal(gathered, n_xy, width, n_grow):
    n_gcol, rows, wide_sub = gathered.shape
    depth = n_gcol * rows // n_xy
    vmem = pl.BlockSpec(memory_space=pltpu.VMEM)
    return pl.pallas_call(
        deal_kernel,
        out_shape=(jax.ShapeDtypeStruct((n_xy, depth, wide_sub), jnp.bfloat16),
                   jax.ShapeDtypeStruct((n_grow, depth, width), jnp.bfloat16)),
        in_specs=[vmem],
        out_specs=(vmem, vmem),
        scratch_shapes=[pltpu.VMEM((-(-wide_sub // LANES), n_gcol * rows, LANES), jnp.float32)],
        compiler_params=pltpu.CompilerParams(vmem_limit_bytes=24 * 1024 * 1024),
        cost_estimate=pl.CostEstimate(flops=10**6, bytes_accessed=2 * 10**6, transcendentals=0),
    )(gathered)


def tile_kernel(row_ref, *refs):
    col_refs, own_ref, sent_refs, total = refs[:NX], refs[NX], refs[NX + 1:-1], refs[-1]
    n_grow, depth, width = col_refs[0].shape
    wide_sub = row_ref.shape[2]
    mine = position("pair") % NX
    value = None
    for step, col_ref in enumerate(col_refs):
        source = (mine + (NX - step)) % NX
        left = row_ref[pl.ds(source * n_grow, n_grow)].reshape(n_grow * depth, wide_sub)
        term = lax.dot_general(
            left, col_ref[...].reshape(n_grow * depth, width), (((0,), (0,)), ((), ())),
            preferred_element_type=jnp.float32)
        value = term if value is None else value + term
    total[...] = value
    sub = own_ref.shape[0]
    layer = position("pair") // NX
    own_ref[...] = total[pl.ds(pl.multiple_of(layer * sub, 8), sub), :]
    for at, sent_ref in enumerate(sent_refs):
        target = (layer + at + 1) % (len(sent_refs) + 1)
        sent_ref[...] = total[pl.ds(pl.multiple_of(target * sub, 8), sub), :].astype(jnp.bfloat16)


def tile(row, cols, n_z):
    n_xy, depth, wide_sub = row.shape
    width = cols[0].shape[2]
    sub = wide_sub // n_z
    vmem = pl.BlockSpec(memory_space=pltpu.VMEM)
    return pl.pallas_call(
        tile_kernel,
        out_shape=[jax.ShapeDtypeStruct((sub, width), jnp.float32)]
        + [jax.ShapeDtypeStruct((sub, width), jnp.bfloat16)] * (n_z - 1),
        in_specs=[vmem] * (1 + NX),
        out_specs=[vmem] * n_z,
        scratch_shapes=[pltpu.VMEM((wide_sub, width), jnp.float32)],
        compiler_params=pltpu.CompilerParams(vmem_limit_bytes=40 * 1024 * 1024),
        cost_estimate=pl.CostEstimate(
            flops=2 * n_xy * depth * wide_sub * width, bytes_accessed=5 * 10**6, transcendentals=0),
    )(row, *cols)


def local(valence, conduction, valence_energy, conduction_energy, pair_valence, pair_conduction,
          pair_count, g_index):
    n_pair, n_grow, n_gcol = (lax.axis_size(name) for name in ("pair", "grow", "gcol"))
    n_z = n_pair // NX
    total_g = g_index.shape[0]
    width = total_g // n_gcol
    sub = total_g // (n_pair * n_grow)
    n_xy = NX * n_grow
    xy_groups = [[(z * NX + x) * n_grow + y for x in range(NX) for y in range(n_grow)]
                 for z in range(n_z)]
    mine = amplitudes_of(
        pair_valence, pair_conduction, pair_count, valence_energy, conduction_energy,
        valence, conduction, g_index, n_xy, n_z * sub)
    mine = lax.all_gather(mine, "gcol", axis=0, tiled=True)
    row, col = deal(mine, n_xy, width, n_grow)
    row = lax.all_to_all(row, ("pair", "grow"), 0, 0, tiled=True, axis_index_groups=xy_groups)
    col = lax.all_to_all(col, "grow", 0, 0, tiled=True)
    cols = [col] + [
        lax.ppermute(col, "pair", [(z * NX + x, z * NX + (x + step) % NX)
                                   for z in range(n_z) for x in range(NX)])
        for step in range(1, NX)]
    own, *sent = tile(row, cols, n_z)
    for step, block in enumerate(sent, 1):
        own = own + lax.ppermute(block, "pair", [(z * NX + x, (z + step) % n_z * NX + x)
                                                 for z in range(n_z) for x in range(NX)])
    total_slots = pair_valence.shape[0] * n_pair * n_grow * n_gcol
    return -own / jnp.sqrt(jnp.float32(total_slots))


def solution(mesh):
    return jax.shard_map(
        local,
        mesh=mesh,
        in_specs=(
            P(),
            P("pair", None),
            P(),
            P("pair"),
            P(("pair", "grow", "gcol")),
            P(("pair", "grow", "gcol")),
            P(("pair", "grow", "gcol")),
            P(),
        ),
        out_specs=P(("pair", "grow"), "gcol"),
        check_vma=False,
    )
```

```python
import numpy as np
import ml_dtypes

import jax
import jax.numpy as jnp
from jax import lax
from jax.experimental import pallas as pl
from jax.experimental.pallas import tpu as pltpu
from jax.sharding import PartitionSpec as P

GRID = 32
NX = 4
LANES = 128
ROWS = 256
CHUNK = 384


def split(table):
    high = table.astype(ml_dtypes.bfloat16)
    low = (table - high.astype(np.float64)).astype(ml_dtypes.bfloat16)
    return high, low


def tables():
    turn = 2.0 * np.pi / GRID
    phase = turn * np.outer(np.arange(32), np.arange(16))
    first = np.concatenate(
        [np.kron(np.eye(4), np.cos(phase)), np.kron(np.eye(4), -np.sin(phase))], axis=1
    )
    high, low = split(first)
    both = np.concatenate([high, low], axis=1)
    lane_table = np.concatenate([both, both], axis=0)
    a_half = np.repeat(np.arange(16), 8)
    beta_half = np.tile(np.arange(8), 16)
    i_row = np.repeat(np.arange(32), 8)
    j_row = np.tile(np.arange(8), 32)
    phase = 2.0 * np.pi * (np.outer(a_half, i_row) / 32.0 + np.outer(beta_half, j_row) / 8.0)
    high, low = split(np.concatenate([np.cos(phase), np.sin(phase)], axis=0))
    row_table = np.concatenate([high, high, low], axis=1)
    beta = np.concatenate([beta_half, (8 - beta_half) % 8])
    angle = turn * np.outer(beta, np.repeat(np.arange(4), 16))
    twiddle_same = np.concatenate([np.cos(angle), np.cos(angle)], axis=1).astype(np.float32)
    twiddle_swap = np.concatenate([np.sin(angle), -np.sin(angle)], axis=1).astype(np.float32)
    step = np.outer(np.arange(4), np.arange(4)) % 4
    real = np.array([1, 0, -1, 0])[step]
    imag = np.array([0, -1, 0, 1])[step]
    last = np.block([[np.kron(real, np.eye(16)), np.kron(imag, np.eye(16))],
                     [np.kron(-imag, np.eye(16)), np.kron(real, np.eye(16))]])
    last_table = np.concatenate([last, last], axis=0).astype(ml_dtypes.bfloat16)
    return lane_table, row_table, twiddle_same, twiddle_swap, last_table


def halves(value):
    high = value.astype(jnp.bfloat16)
    low = (value - high.astype(jnp.float32)).astype(jnp.bfloat16)
    return high, low


def position(name):
    return lax.axis_index(name)


def dot(left, right):
    return jnp.dot(left, right, preferred_element_type=jnp.float32)


def select(cells, amplitudes):
    first = cells >> 10
    second = (cells >> 5) & 31
    third = cells & 31
    flip = third >= 16
    first = jnp.where(flip, (32 - first) & 31, first)
    second = jnp.where(flip, (32 - second) & 31, second)
    third = jnp.where(flip, 32 - third, third)
    sign = jnp.where(flip, -1.0, 1.0)
    beta = second & 7
    row = jnp.where(
        first > 16, 128 + (32 - first) * 8 + ((8 - beta) & 7), first * 8 + beta
    )
    lane = (second >> 3) * 16 + third
    width = cells.shape[-1]
    row_id = lax.broadcasted_iota(jnp.int32, (ROWS, width), 0).astype(jnp.bfloat16)
    one, zero = jnp.ones((), jnp.bfloat16), jnp.zeros((), jnp.bfloat16)
    hot = jnp.where(row_id == row.astype(jnp.bfloat16), one, zero)
    picked = dot(amplitudes, hot)
    mask = lax.broadcasted_iota(jnp.int32, (64, width), 0) == lane
    parts = []
    for part in range(4):
        block = jnp.where(mask, picked[part * 64:part * 64 + 64], 0.0)
        total = jnp.sum(block, axis=0, keepdims=True)
        parts.append(total * sign if part % 2 else total)
    return jnp.concatenate(parts, axis=0)


def lane_tiles(width):
    return [(lane, min(LANES, width - lane)) for lane in range(0, width, LANES)]


def amplitude_kernel(pv_hbm, pc_hbm, count_hbm, ve_hbm, ce_hbm, valence_hbm, conduction_hbm,
                     lane_hbm, row_hbm, same_hbm, swap_hbm, last_hbm, g_hbm,
                     col_ref, rows_ref, pv_ref, pc_ref, count_ref, ve_ref, ce_ref, valence_ref,
                     conduction_ref, lane_ref, row_ref, same_ref, swap_ref, last_ref, g_ref,
                     wide, amp, flat, sems):
    slots = 2
    n_xy, doubled, wide_sub = rows_ref.shape
    sub = wide_sub // 3
    width = col_ref.shape[2]
    sources = (pv_hbm, pc_hbm, conduction_hbm, valence_hbm, lane_hbm, row_hbm, same_hbm,
               swap_hbm, last_hbm, g_hbm, count_hbm, ve_hbm, ce_hbm)
    targets = (pv_ref, pc_ref, conduction_ref, valence_ref, lane_ref, row_ref, same_ref,
               swap_ref, last_ref, g_ref, count_ref, ve_ref, ce_ref)
    copies = [pltpu.make_async_copy(source, target, sems.at[at])
              for at, (source, target) in enumerate(zip(sources, targets))]
    for copy in copies:
        copy.start()
    for copy in copies[:4]:
        copy.wait()
    picks = [(valence_ref, pv_ref[slot]) for slot in range(slots)]
    picks += [(conduction_ref, pc_ref[slot]) for slot in range(slots)]

    def widen(tile, carry):
        lanes = pl.ds(pl.multiple_of(tile * LANES, LANES), LANES)
        rows = pl.ds(pl.multiple_of(tile * 8, 8), 8)
        for at, (ref, band) in enumerate(picks):
            start = pl.multiple_of(band // 16 * 16, 16)
            block = ref[pl.ds(start, 16), lanes].astype(jnp.float32)
            wide[at, rows, :] = jnp.where(band % 16 >= 8, block[8:], block[:8])
        return carry

    lax.fori_loop(0, ROWS, widen, 0, unroll=8)
    for copy in copies[4:]:
        copy.wait()

    stage = []
    for slot in range(slots):
        left = wide[slot, pl.ds(pv_ref[slot] % 8, ROWS, stride=8), :]
        right = wide[slots + slot, pl.ds(pc_ref[slot] % 8, ROWS, stride=8), :]
        high, low = halves(left * right)
        out = dot(jnp.concatenate([high, low], axis=1), lane_ref[...])
        stage.append(out[:, :LANES] + out[:, LANES:])
    high, low = halves(jnp.concatenate(stage, axis=1))
    out = dot(row_ref[...], jnp.concatenate([high, low, high], axis=0))
    lane_id = lax.broadcasted_iota(jnp.int32, (LANES, LANES), 1)
    for slot in range(slots):
        lanes = slice(slot * LANES, slot * LANES + LANES)
        cosine, sine = out[:LANES, lanes], out[LANES:, lanes]
        turned = pltpu.roll(sine, 64, 1)
        turned = jnp.where(lane_id < 64, turned, -turned)
        full = jnp.concatenate([cosine + turned, cosine - turned], axis=0)
        full = full * same_ref[...] + pltpu.roll(full, 64, 1) * swap_ref[...]
        high, low = halves(full)
        spectrum = dot(jnp.concatenate([high, low], axis=1), last_ref[...])
        gap = ce_ref[pc_ref[slot]] - ve_ref[pv_ref[slot]]
        live = jnp.where(slot < count_ref[0], 1.0, 0.0)
        factor = live * jnp.sqrt(4.0 / jnp.full((1, LANES), gap, jnp.float32)) / np.float32(
            np.sqrt(np.float32(GRID**3)))
        amp[slot * LANES:slot * LANES + LANES, :] = (spectrum * factor).T.astype(jnp.bfloat16)

    per = CHUNK // LANES

    def pick(chunk, carry):
        cells = jnp.concatenate(
            [g_ref[pl.ds(chunk * per + at, 1), :] for at in range(per)], axis=1)
        lanes = pl.ds(pl.multiple_of(chunk * CHUNK, CHUNK), CHUNK)
        flat[0:4, lanes] = select(cells, amp[...])
        return carry

    lax.fori_loop(0, flat.shape[1] // CHUNK, pick, 0, unroll=3)
    for place in range(n_xy):
        starts = [(z * n_xy + place) * sub for z in range(3)]
        block = jnp.concatenate([flat[0:doubled, at:at + sub] for at in starts], axis=1)
        rows_ref[place] = block.astype(jnp.bfloat16)
    for target in range(col_ref.shape[0]):
        col_ref[target] = flat[0:doubled, target * width:(target + 1) * width].astype(jnp.bfloat16)


def amplitudes_of(pv, pc, count, ve, ce, valence, conduction, g_index, n_xy, wide_sub, n_gcol):
    hbm = pl.BlockSpec(memory_space=pltpu.HBM)
    consts = [jnp.asarray(table) for table in tables()]
    g_rows = g_index.reshape(-1, LANES)
    arrays = [valence, conduction, *consts, g_rows]
    doubled = 2 * pv.shape[0]
    return pl.pallas_call(
        amplitude_kernel,
        out_shape=(
            jax.ShapeDtypeStruct((n_gcol, doubled, g_index.shape[0] // n_gcol), jnp.bfloat16),
            jax.ShapeDtypeStruct((n_xy, doubled, wide_sub), jnp.bfloat16)),
        in_specs=[hbm] * 13,
        out_specs=(pl.BlockSpec(memory_space=pltpu.VMEM),) * 2,
        scratch_shapes=[pltpu.SMEM(a.shape, a.dtype) for a in (pv, pc, count, ve, ce)]
        + [pltpu.VMEM(a.shape, a.dtype) for a in arrays]
        + [
            pltpu.VMEM((4, 8 * ROWS, LANES), jnp.float32),
            pltpu.VMEM((ROWS, ROWS), jnp.bfloat16),
            pltpu.VMEM((8, g_index.shape[0]), jnp.float32),
            pltpu.SemaphoreType.DMA((13,)),
        ],
        compiler_params=pltpu.CompilerParams(vmem_limit_bytes=60 * 1024 * 1024),
        cost_estimate=pl.CostEstimate(flops=4 * 10**9, bytes_accessed=5 * 10**6, transcendentals=0),
    )(pv, pc, count, ve, ce, *arrays)


def spread_kernel(in_ref, first_ref, out_ref, wide):
    del first_ref
    n_gcol, doubled, width = in_ref.shape
    for at in range(n_gcol):
        block = in_ref[at].astype(jnp.float32)
        for lane in range(width // LANES):
            wide[lane, pl.ds(at, doubled, stride=n_gcol), :] = block[
                :, lane * LANES:(lane + 1) * LANES]
    for lane in range(width // LANES):
        block = wide[lane].astype(jnp.bfloat16)
        for target in range(out_ref.shape[0]):
            out_ref[target, :, lane * LANES:(lane + 1) * LANES] = block


def spread(col, first, n_grow):
    n_gcol, doubled, width = col.shape
    vmem = pl.BlockSpec(memory_space=pltpu.VMEM)
    return pl.pallas_call(
        spread_kernel,
        out_shape=jax.ShapeDtypeStruct((n_grow, n_gcol * doubled, width), jnp.bfloat16),
        in_specs=[vmem, pl.BlockSpec(memory_space=pl.ANY)],
        out_specs=vmem,
        scratch_shapes=[pltpu.VMEM((width // LANES, n_gcol * doubled, LANES), jnp.float32)],
        compiler_params=pltpu.CompilerParams(vmem_limit_bytes=16 * 1024 * 1024),
        cost_estimate=pl.CostEstimate(flops=10**6, bytes_accessed=2 * 10**6, transcendentals=0),
    )(col, first)


def tile_kernel(row_ref, *refs):
    col_refs, own_ref, sent_refs = refs[:NX], refs[NX], refs[NX + 1:-2]
    wide, total = refs[-2:]
    n_grow, depth, width = col_refs[0].shape
    n_gcol, stride, wide_sub = row_ref.shape
    doubled = depth // n_gcol
    tiles = lane_tiles(wide_sub)
    for at, (lane, size) in enumerate(tiles):
        block = row_ref[:, :, lane:lane + size].astype(jnp.float32)
        wide[at, :, :size] = block.reshape(n_gcol * stride, size)
    mine = position("pair") % NX
    value = None
    for step, col_ref in enumerate(col_refs):
        first = (mine + (NX - step)) % NX * (n_grow * doubled)
        left = jnp.concatenate(
            [jnp.concatenate([wide[at, pl.ds(first + place, n_gcol, stride=stride), :]
                              for place in range(n_grow * doubled)], axis=0)
             for at in range(len(tiles))], axis=1)[:, :wide_sub].astype(jnp.bfloat16)
        term = lax.dot_general(
            left, col_ref[...].reshape(n_grow * depth, width), (((0,), (0,)), ((), ())),
            preferred_element_type=jnp.float32)
        value = term if value is None else value + term
    total[...] = value
    sub = own_ref.shape[0]
    layer = position("pair") // NX
    own_ref[...] = total[pl.ds(pl.multiple_of(layer * sub, 8), sub), :]
    for at, sent_ref in enumerate(sent_refs):
        target = (layer + at + 1) % (len(sent_refs) + 1)
        sent_ref[...] = total[pl.ds(pl.multiple_of(target * sub, 8), sub), :].astype(jnp.bfloat16)


def tile(row, cols, n_z):
    n_gcol, rows, wide_sub = row.shape
    width = cols[0].shape[2]
    sub = wide_sub // n_z
    vmem = pl.BlockSpec(memory_space=pltpu.VMEM)
    return pl.pallas_call(
        tile_kernel,
        out_shape=[jax.ShapeDtypeStruct((sub, width), jnp.float32)]
        + [jax.ShapeDtypeStruct((sub, width), jnp.bfloat16)] * (n_z - 1),
        in_specs=[vmem] * (1 + NX),
        out_specs=[vmem] * n_z,
        scratch_shapes=[pltpu.VMEM((-(-wide_sub // LANES), n_gcol * rows, LANES), jnp.float32),
                        pltpu.VMEM((wide_sub, width), jnp.float32)],
        compiler_params=pltpu.CompilerParams(vmem_limit_bytes=40 * 1024 * 1024),
        cost_estimate=pl.CostEstimate(
            flops=2 * n_gcol * rows * wide_sub * width, bytes_accessed=5 * 10**6, transcendentals=0),
    )(row, *cols)


def local(valence, conduction, valence_energy, conduction_energy, pair_valence, pair_conduction,
          pair_count, g_index):
    n_pair, n_grow, n_gcol = (lax.axis_size(name) for name in ("pair", "grow", "gcol"))
    n_z = n_pair // NX
    total_g = g_index.shape[0]
    width = total_g // n_gcol
    sub = total_g // (n_pair * n_grow)
    n_xy = NX * n_grow
    xy_groups = [[(z * NX + x) * n_grow + y for x in range(NX) for y in range(n_grow)]
                 for z in range(n_z)]
    col, row = amplitudes_of(
        pair_valence, pair_conduction, pair_count, valence_energy, conduction_energy,
        valence, conduction, g_index, n_xy, n_z * sub, n_gcol)
    row = lax.all_to_all(row, ("pair", "grow"), 0, 0, tiled=True, axis_index_groups=xy_groups)
    col = spread(lax.all_to_all(col, "gcol", 0, 0, tiled=True), row, n_grow)
    col = lax.all_to_all(col, "grow", 0, 0, tiled=True)
    row = lax.all_gather(row.reshape(1, -1, n_z * sub), "gcol", axis=0, tiled=True)
    cols = [col] + [
        lax.ppermute(col, "pair", [(z * NX + x, z * NX + (x + step) % NX)
                                   for z in range(n_z) for x in range(NX)])
        for step in range(1, NX)]
    own, *sent = tile(row, cols, n_z)
    for step, block in enumerate(sent, 1):
        own = own + lax.ppermute(block, "pair", [(z * NX + x, (z + step) % n_z * NX + x)
                                                 for z in range(n_z) for x in range(NX)])
    total_slots = pair_valence.shape[0] * n_pair * n_grow * n_gcol
    return -own / jnp.sqrt(jnp.float32(total_slots))


def solution(mesh):
    return jax.shard_map(
        local,
        mesh=mesh,
        in_specs=(
            P(),
            P("pair", None),
            P(),
            P("pair"),
            P(("pair", "grow", "gcol")),
            P(("pair", "grow", "gcol")),
            P(("pair", "grow", "gcol")),
            P(),
        ),
        out_specs=P(("pair", "grow"), "gcol"),
        check_vma=False,
    )
```

```python
import numpy as np
import ml_dtypes

import jax
import jax.numpy as jnp
from jax import lax
from jax.experimental import pallas as pl
from jax.experimental.pallas import tpu as pltpu
from jax.sharding import PartitionSpec as P

GRID = 32
NX = 4
LANES = 128
ROWS = 256
CHUNK = 384


def split(table):
    high = table.astype(ml_dtypes.bfloat16)
    low = (table - high.astype(np.float64)).astype(ml_dtypes.bfloat16)
    return high, low


def tables():
    turn = 2.0 * np.pi / GRID
    phase = turn * np.outer(np.arange(32), np.arange(16))
    first = np.concatenate(
        [np.kron(np.eye(4), np.cos(phase)), np.kron(np.eye(4), -np.sin(phase))], axis=1
    )
    high, low = split(first)
    both = np.concatenate([high, low], axis=1)
    lane_table = np.concatenate([both, both], axis=0)
    a_half = np.repeat(np.arange(16), 8)
    beta_half = np.tile(np.arange(8), 16)
    i_row = np.repeat(np.arange(32), 8)
    j_row = np.tile(np.arange(8), 32)
    phase = 2.0 * np.pi * (np.outer(a_half, i_row) / 32.0 + np.outer(beta_half, j_row) / 8.0)
    high, low = split(np.concatenate([np.cos(phase), np.sin(phase)], axis=0))
    row_table = np.concatenate([high, high, low], axis=1)
    beta = np.concatenate([beta_half, (8 - beta_half) % 8])
    angle = turn * np.outer(beta, np.repeat(np.arange(4), 16))
    twiddle_same = np.concatenate([np.cos(angle), np.cos(angle)], axis=1).astype(np.float32)
    twiddle_swap = np.concatenate([np.sin(angle), -np.sin(angle)], axis=1).astype(np.float32)
    step = np.outer(np.arange(4), np.arange(4)) % 4
    real = np.array([1, 0, -1, 0])[step]
    imag = np.array([0, -1, 0, 1])[step]
    last = np.block([[np.kron(real, np.eye(16)), np.kron(imag, np.eye(16))],
                     [np.kron(-imag, np.eye(16)), np.kron(real, np.eye(16))]])
    last_table = np.concatenate([last, last], axis=0).astype(ml_dtypes.bfloat16)
    return lane_table, row_table, twiddle_same, twiddle_swap, last_table


def halves(value):
    high = value.astype(jnp.bfloat16)
    low = (value - high.astype(jnp.float32)).astype(jnp.bfloat16)
    return high, low


def position(name):
    return lax.axis_index(name)


def dot(left, right):
    return jnp.dot(left, right, preferred_element_type=jnp.float32)


def select(cells, amplitudes):
    first = cells >> 10
    second = (cells >> 5) & 31
    third = cells & 31
    flip = third >= 16
    first = jnp.where(flip, (32 - first) & 31, first)
    second = jnp.where(flip, (32 - second) & 31, second)
    third = jnp.where(flip, 32 - third, third)
    sign = jnp.where(flip, -1.0, 1.0)
    beta = second & 7
    row = jnp.where(
        first > 16, 128 + (32 - first) * 8 + ((8 - beta) & 7), first * 8 + beta
    )
    lane = (second >> 3) * 16 + third
    width = cells.shape[-1]
    row_id = lax.broadcasted_iota(jnp.int32, (ROWS, width), 0).astype(jnp.bfloat16)
    one, zero = jnp.ones((), jnp.bfloat16), jnp.zeros((), jnp.bfloat16)
    hot = jnp.where(row_id == row.astype(jnp.bfloat16), one, zero)
    picked = dot(amplitudes, hot)
    mask = lax.broadcasted_iota(jnp.int32, (64, width), 0) == lane
    parts = []
    for part in range(4):
        block = jnp.where(mask, picked[part * 64:part * 64 + 64], 0.0)
        total = jnp.sum(block, axis=0, keepdims=True)
        parts.append(total * sign if part % 2 else total)
    return jnp.concatenate(parts, axis=0)


def lane_tiles(width):
    return [(lane, min(LANES, width - lane)) for lane in range(0, width, LANES)]


def amplitude_kernel(pv_hbm, pc_hbm, count_hbm, ve_hbm, ce_hbm, valence_hbm, conduction_hbm,
                     lane_hbm, row_hbm, same_hbm, swap_hbm, last_hbm, g_hbm,
                     col_ref, rows_ref, pv_ref, pc_ref, count_ref, ve_ref, ce_ref, valence_ref,
                     conduction_ref, lane_ref, row_ref, same_ref, swap_ref, last_ref, g_ref,
                     wide, amp, flat, ordered, sems):
    slots = 2
    n_xy, doubled, wide_sub = rows_ref.shape
    sub = wide_sub // 3
    width = col_ref.shape[2]
    sources = (pv_hbm, pc_hbm, conduction_hbm, valence_hbm, lane_hbm, row_hbm, same_hbm,
               swap_hbm, last_hbm, g_hbm, count_hbm, ve_hbm, ce_hbm)
    targets = (pv_ref, pc_ref, conduction_ref, valence_ref, lane_ref, row_ref, same_ref,
               swap_ref, last_ref, g_ref, count_ref, ve_ref, ce_ref)
    copies = [pltpu.make_async_copy(source, target, sems.at[at])
              for at, (source, target) in enumerate(zip(sources, targets))]
    for copy in copies:
        copy.start()
    for copy in copies[:4]:
        copy.wait()
    picks = [(valence_ref, pv_ref[slot]) for slot in range(slots)]
    picks += [(conduction_ref, pc_ref[slot]) for slot in range(slots)]

    def widen(tile, carry):
        lanes = pl.ds(pl.multiple_of(tile * LANES, LANES), LANES)
        rows = pl.ds(pl.multiple_of(tile * 8, 8), 8)
        for at, (ref, band) in enumerate(picks):
            start = pl.multiple_of(band // 16 * 16, 16)
            block = ref[pl.ds(start, 16), lanes].astype(jnp.float32)
            wide[at, rows, :] = jnp.where(band % 16 >= 8, block[8:], block[:8])
        return carry

    lax.fori_loop(0, ROWS, widen, 0, unroll=8)
    for copy in copies[4:]:
        copy.wait()

    stage = []
    for slot in range(slots):
        left = wide[slot, pl.ds(pv_ref[slot] % 8, ROWS, stride=8), :]
        right = wide[slots + slot, pl.ds(pc_ref[slot] % 8, ROWS, stride=8), :]
        high, low = halves(left * right)
        out = dot(jnp.concatenate([high, low], axis=1), lane_ref[...])
        stage.append(out[:, :LANES] + out[:, LANES:])
    high, low = halves(jnp.concatenate(stage, axis=1))
    out = dot(row_ref[...], jnp.concatenate([high, low, high], axis=0))
    lane_id = lax.broadcasted_iota(jnp.int32, (LANES, LANES), 1)
    for slot in range(slots):
        lanes = slice(slot * LANES, slot * LANES + LANES)
        cosine, sine = out[:LANES, lanes], out[LANES:, lanes]
        turned = pltpu.roll(sine, 64, 1)
        turned = jnp.where(lane_id < 64, turned, -turned)
        full = jnp.concatenate([cosine + turned, cosine - turned], axis=0)
        full = full * same_ref[...] + pltpu.roll(full, 64, 1) * swap_ref[...]
        high, low = halves(full)
        spectrum = dot(jnp.concatenate([high, low], axis=1), last_ref[...])
        gap = ce_ref[pc_ref[slot]] - ve_ref[pv_ref[slot]]
        live = jnp.where(slot < count_ref[0], 1.0, 0.0)
        factor = live * jnp.sqrt(4.0 / jnp.full((1, LANES), gap, jnp.float32)) / np.float32(
            np.sqrt(np.float32(GRID**3)))
        amp[slot * LANES:slot * LANES + LANES, :] = (spectrum * factor).T.astype(jnp.bfloat16)

    per = CHUNK // LANES

    def pick(chunk, carry):
        cells = jnp.concatenate(
            [g_ref[pl.ds(chunk * per + at, 1), :] for at in range(per)], axis=1)
        lanes = pl.ds(pl.multiple_of(chunk * CHUNK, CHUNK), CHUNK)
        flat[0:4, lanes] = select(cells, amp[...])
        return carry

    lax.fori_loop(0, flat.shape[1] // CHUNK, pick, 0, unroll=3)
    for place in range(n_xy):
        starts = [(z * n_xy + place) * sub for z in range(3)]
        block = jnp.concatenate([flat[0:doubled, at:at + sub] for at in starts], axis=1)
        rows_ref[place] = block.astype(jnp.bfloat16)
    targets = flat.shape[1] // width
    for at in range(width // LANES):
        for target in range(targets):
            lane = target * width + at * LANES
            ordered[at, pl.ds(target, doubled, stride=targets), :] = flat[
                0:doubled, lane:lane + LANES]
        col_ref[0, :, at * LANES:(at + 1) * LANES] = ordered[at].astype(jnp.bfloat16)


def amplitudes_of(pv, pc, count, ve, ce, valence, conduction, g_index, n_xy, wide_sub, n_gcol):
    hbm = pl.BlockSpec(memory_space=pltpu.HBM)
    consts = [jnp.asarray(table) for table in tables()]
    g_rows = g_index.reshape(-1, LANES)
    arrays = [valence, conduction, *consts, g_rows]
    doubled = 2 * pv.shape[0]
    width = g_index.shape[0] // n_gcol
    return pl.pallas_call(
        amplitude_kernel,
        out_shape=(
            jax.ShapeDtypeStruct((1, doubled * n_gcol, width), jnp.bfloat16),
            jax.ShapeDtypeStruct((n_xy, doubled, wide_sub), jnp.bfloat16)),
        in_specs=[hbm] * 13,
        out_specs=(pl.BlockSpec(memory_space=pltpu.VMEM),) * 2,
        scratch_shapes=[pltpu.SMEM(a.shape, a.dtype) for a in (pv, pc, count, ve, ce)]
        + [pltpu.VMEM(a.shape, a.dtype) for a in arrays]
        + [
            pltpu.VMEM((4, 8 * ROWS, LANES), jnp.float32),
            pltpu.VMEM((ROWS, ROWS), jnp.bfloat16),
            pltpu.VMEM((8, g_index.shape[0]), jnp.float32),
            pltpu.VMEM((width // LANES, doubled * n_gcol, LANES), jnp.float32),
            pltpu.SemaphoreType.DMA((13,)),
        ],
        compiler_params=pltpu.CompilerParams(vmem_limit_bytes=60 * 1024 * 1024),
        cost_estimate=pl.CostEstimate(flops=4 * 10**9, bytes_accessed=5 * 10**6, transcendentals=0),
    )(pv, pc, count, ve, ce, *arrays)


def spread_kernel(in_ref, first_ref, out_ref, wide):
    del first_ref
    n_gcol, depth, width = in_ref.shape
    mine = position("gcol")
    for at in range(width // LANES):
        lanes = slice(at * LANES, (at + 1) * LANES)
        wide[at] = in_ref[:, :, lanes].astype(jnp.float32).reshape(n_gcol * depth, LANES)
        block = jnp.concatenate(
            [wide[at, pl.ds(row * n_gcol + mine, n_gcol, stride=depth), :]
             for row in range(depth // n_gcol)], axis=0).astype(jnp.bfloat16)
        for target in range(out_ref.shape[0]):
            out_ref[target, :, lanes] = block


def spread(col, first, n_grow):
    n_gcol, depth, width = col.shape
    vmem = pl.BlockSpec(memory_space=pltpu.VMEM)
    return pl.pallas_call(
        spread_kernel,
        out_shape=jax.ShapeDtypeStruct((n_grow, depth, width), jnp.bfloat16),
        in_specs=[vmem, pl.BlockSpec(memory_space=pl.ANY)],
        out_specs=vmem,
        scratch_shapes=[pltpu.VMEM((width // LANES, n_gcol * depth, LANES), jnp.float32)],
        compiler_params=pltpu.CompilerParams(vmem_limit_bytes=16 * 1024 * 1024),
        cost_estimate=pl.CostEstimate(flops=10**6, bytes_accessed=2 * 10**6, transcendentals=0),
    )(col, first)


def tile_kernel(row_ref, *refs):
    col_refs, own_ref, sent_refs = refs[:NX], refs[NX], refs[NX + 1:-2]
    wide, total = refs[-2:]
    n_grow, depth, width = col_refs[0].shape
    n_gcol, stride, wide_sub = row_ref.shape
    doubled = depth // n_gcol
    tiles = lane_tiles(wide_sub)
    for at, (lane, size) in enumerate(tiles):
        block = row_ref[:, :, lane:lane + size].astype(jnp.float32)
        wide[at, :, :size] = block.reshape(n_gcol * stride, size)
    mine = position("pair") % NX
    value = None
    for step, col_ref in enumerate(col_refs):
        first = (mine + (NX - step)) % NX * (n_grow * doubled)
        left = jnp.concatenate(
            [jnp.concatenate([wide[at, pl.ds(first + place, n_gcol, stride=stride), :]
                              for place in range(n_grow * doubled)], axis=0)
             for at in range(len(tiles))], axis=1)[:, :wide_sub].astype(jnp.bfloat16)
        term = lax.dot_general(
            left, col_ref[...].reshape(n_grow * depth, width), (((0,), (0,)), ((), ())),
            preferred_element_type=jnp.float32)
        value = term if value is None else value + term
    total[...] = value
    sub = own_ref.shape[0]
    layer = position("pair") // NX
    own_ref[...] = total[pl.ds(pl.multiple_of(layer * sub, 8), sub), :]
    for at, sent_ref in enumerate(sent_refs):
        target = (layer + at + 1) % (len(sent_refs) + 1)
        sent_ref[...] = total[pl.ds(pl.multiple_of(target * sub, 8), sub), :].astype(jnp.bfloat16)


def tile(row, cols, n_z):
    n_gcol, rows, wide_sub = row.shape
    width = cols[0].shape[2]
    sub = wide_sub // n_z
    vmem = pl.BlockSpec(memory_space=pltpu.VMEM)
    return pl.pallas_call(
        tile_kernel,
        out_shape=[jax.ShapeDtypeStruct((sub, width), jnp.float32)]
        + [jax.ShapeDtypeStruct((sub, width), jnp.bfloat16)] * (n_z - 1),
        in_specs=[vmem] * (1 + NX),
        out_specs=[vmem] * n_z,
        scratch_shapes=[pltpu.VMEM((-(-wide_sub // LANES), n_gcol * rows, LANES), jnp.float32),
                        pltpu.VMEM((wide_sub, width), jnp.float32)],
        compiler_params=pltpu.CompilerParams(vmem_limit_bytes=40 * 1024 * 1024),
        cost_estimate=pl.CostEstimate(
            flops=2 * n_gcol * rows * wide_sub * width, bytes_accessed=5 * 10**6, transcendentals=0),
    )(row, *cols)


def local(valence, conduction, valence_energy, conduction_energy, pair_valence, pair_conduction,
          pair_count, g_index):
    n_pair, n_grow, n_gcol = (lax.axis_size(name) for name in ("pair", "grow", "gcol"))
    n_z = n_pair // NX
    total_g = g_index.shape[0]
    width = total_g // n_gcol
    sub = total_g // (n_pair * n_grow)
    n_xy = NX * n_grow
    xy_groups = [[(z * NX + x) * n_grow + y for x in range(NX) for y in range(n_grow)]
                 for z in range(n_z)]
    col, row = amplitudes_of(
        pair_valence, pair_conduction, pair_count, valence_energy, conduction_energy,
        valence, conduction, g_index, n_xy, n_z * sub, n_gcol)
    row = lax.all_to_all(row, ("pair", "grow"), 0, 0, tiled=True, axis_index_groups=xy_groups)
    col = spread(lax.all_gather(col, "gcol", axis=0, tiled=True), row, n_grow)
    col = lax.all_to_all(col, "grow", 0, 0, tiled=True)
    row = lax.all_gather(row.reshape(1, -1, n_z * sub), "gcol", axis=0, tiled=True)
    cols = [col] + [
        lax.ppermute(col, "pair", [(z * NX + x, z * NX + (x + step) % NX)
                                   for z in range(n_z) for x in range(NX)])
        for step in range(1, NX)]
    own, *sent = tile(row, cols, n_z)
    for step, block in enumerate(sent, 1):
        own = own + lax.ppermute(block, "pair", [(z * NX + x, (z + step) % n_z * NX + x)
                                                 for z in range(n_z) for x in range(NX)])
    total_slots = pair_valence.shape[0] * n_pair * n_grow * n_gcol
    return -own / jnp.sqrt(jnp.float32(total_slots))


def solution(mesh):
    return jax.shard_map(
        local,
        mesh=mesh,
        in_specs=(
            P(),
            P("pair", None),
            P(),
            P("pair"),
            P(("pair", "grow", "gcol")),
            P(("pair", "grow", "gcol")),
            P(("pair", "grow", "gcol")),
            P(),
        ),
        out_specs=P(("pair", "grow"), "gcol"),
        check_vma=False,
    )
```

```python
import numpy as np
import ml_dtypes

import jax
import jax.numpy as jnp
from jax import lax
from jax.experimental import pallas as pl
from jax.experimental.pallas import tpu as pltpu
from jax.sharding import PartitionSpec as P

GRID = 32
NX = 4
LANES = 128
ROWS = 256
CHUNK = 384


def split(table):
    high = table.astype(ml_dtypes.bfloat16)
    low = (table - high.astype(np.float64)).astype(ml_dtypes.bfloat16)
    return high, low


def tables():
    turn = 2.0 * np.pi / GRID
    phase = turn * np.outer(np.arange(32), np.arange(16))
    first = np.concatenate(
        [np.kron(np.eye(4), np.cos(phase)), np.kron(np.eye(4), -np.sin(phase))], axis=1
    )
    high, low = split(first)
    both = np.concatenate([high, low], axis=1)
    lane_table = np.concatenate([both, both], axis=0)
    a_half = np.repeat(np.arange(16), 8)
    beta_half = np.tile(np.arange(8), 16)
    i_row = np.repeat(np.arange(32), 8)
    j_row = np.tile(np.arange(8), 32)
    phase = 2.0 * np.pi * (np.outer(a_half, i_row) / 32.0 + np.outer(beta_half, j_row) / 8.0)
    high, low = split(np.concatenate([np.cos(phase), np.sin(phase)], axis=0))
    row_table = np.concatenate([high, high, low], axis=1)
    beta = np.concatenate([beta_half, (8 - beta_half) % 8])
    angle = turn * np.outer(beta, np.repeat(np.arange(4), 16))
    twiddle_same = np.concatenate([np.cos(angle), np.cos(angle)], axis=1).astype(np.float32)
    twiddle_swap = np.concatenate([np.sin(angle), -np.sin(angle)], axis=1).astype(np.float32)
    step = np.outer(np.arange(4), np.arange(4)) % 4
    real = np.array([1, 0, -1, 0])[step]
    imag = np.array([0, -1, 0, 1])[step]
    last = np.block([[np.kron(real, np.eye(16)), np.kron(imag, np.eye(16))],
                     [np.kron(-imag, np.eye(16)), np.kron(real, np.eye(16))]])
    last_table = np.concatenate([last, last], axis=0).astype(ml_dtypes.bfloat16)
    return lane_table, row_table, twiddle_same, twiddle_swap, last_table


def halves(value):
    high = value.astype(jnp.bfloat16)
    low = (value - high.astype(jnp.float32)).astype(jnp.bfloat16)
    return high, low


def position(name):
    return lax.axis_index(name)


def dot(left, right):
    return jnp.dot(left, right, preferred_element_type=jnp.float32)


def select(cells, amplitudes):
    first = cells >> 10
    second = (cells >> 5) & 31
    third = cells & 31
    flip = third >= 16
    first = jnp.where(flip, (32 - first) & 31, first)
    second = jnp.where(flip, (32 - second) & 31, second)
    third = jnp.where(flip, 32 - third, third)
    sign = jnp.where(flip, -1.0, 1.0)
    beta = second & 7
    row = jnp.where(
        first > 16, 128 + (32 - first) * 8 + ((8 - beta) & 7), first * 8 + beta
    )
    lane = (second >> 3) * 16 + third
    width = cells.shape[-1]
    row_id = lax.broadcasted_iota(jnp.int32, (ROWS, width), 0).astype(jnp.bfloat16)
    one, zero = jnp.ones((), jnp.bfloat16), jnp.zeros((), jnp.bfloat16)
    hot = jnp.where(row_id == row.astype(jnp.bfloat16), one, zero)
    picked = dot(amplitudes, hot)
    mask = lax.broadcasted_iota(jnp.int32, (64, width), 0) == lane
    parts = []
    for part in range(4):
        block = jnp.where(mask, picked[part * 64:part * 64 + 64], 0.0)
        total = jnp.sum(block, axis=0, keepdims=True)
        parts.append(total * sign if part % 2 else total)
    return jnp.concatenate(parts, axis=0)


def lane_tiles(width):
    return [(lane, min(LANES, width - lane)) for lane in range(0, width, LANES)]


def amplitude_kernel(pv_hbm, pc_hbm, count_hbm, ve_hbm, ce_hbm, valence_hbm, conduction_hbm,
                     lane_hbm, row_hbm, same_hbm, swap_hbm, last_hbm, g_hbm,
                     col_ref, rows_ref, pv_ref, pc_ref, count_ref, ve_ref, ce_ref, valence_ref,
                     conduction_ref, lane_ref, row_ref, same_ref, swap_ref, last_ref, g_ref,
                     wide, amp, flat, ordered, sems):
    slots = 2
    n_xy, doubled, wide_sub = rows_ref.shape
    sub = wide_sub // 3
    width = col_ref.shape[2]
    sources = (pv_hbm, pc_hbm, conduction_hbm, valence_hbm, lane_hbm, row_hbm, same_hbm,
               swap_hbm, last_hbm, g_hbm, count_hbm, ve_hbm, ce_hbm)
    targets = (pv_ref, pc_ref, conduction_ref, valence_ref, lane_ref, row_ref, same_ref,
               swap_ref, last_ref, g_ref, count_ref, ve_ref, ce_ref)
    copies = [pltpu.make_async_copy(source, target, sems.at[at])
              for at, (source, target) in enumerate(zip(sources, targets))]
    for copy in copies:
        copy.start()
    for copy in copies[:4]:
        copy.wait()
    picks = [(valence_ref, pv_ref[slot]) for slot in range(slots)]
    picks += [(conduction_ref, pc_ref[slot]) for slot in range(slots)]

    def widen(tile, carry):
        lanes = pl.ds(pl.multiple_of(tile * LANES, LANES), LANES)
        rows = pl.ds(pl.multiple_of(tile * 8, 8), 8)
        for at, (ref, band) in enumerate(picks):
            start = pl.multiple_of(band // 16 * 16, 16)
            block = ref[pl.ds(start, 16), lanes].astype(jnp.float32)
            wide[at, rows, :] = jnp.where(band % 16 >= 8, block[8:], block[:8])
        return carry

    lax.fori_loop(0, ROWS, widen, 0, unroll=8)
    for copy in copies[4:]:
        copy.wait()

    stage = []
    for slot in range(slots):
        left = wide[slot, pl.ds(pv_ref[slot] % 8, ROWS, stride=8), :]
        right = wide[slots + slot, pl.ds(pc_ref[slot] % 8, ROWS, stride=8), :]
        high, low = halves(left * right)
        out = dot(jnp.concatenate([high, low], axis=1), lane_ref[...])
        stage.append(out[:, :LANES] + out[:, LANES:])
    high, low = halves(jnp.concatenate(stage, axis=1))
    out = dot(row_ref[...], jnp.concatenate([high, low, high], axis=0))
    lane_id = lax.broadcasted_iota(jnp.int32, (LANES, LANES), 1)
    for slot in range(slots):
        lanes = slice(slot * LANES, slot * LANES + LANES)
        cosine, sine = out[:LANES, lanes], out[LANES:, lanes]
        turned = pltpu.roll(sine, 64, 1)
        turned = jnp.where(lane_id < 64, turned, -turned)
        full = jnp.concatenate([cosine + turned, cosine - turned], axis=0)
        full = full * same_ref[...] + pltpu.roll(full, 64, 1) * swap_ref[...]
        high, low = halves(full)
        spectrum = dot(jnp.concatenate([high, low], axis=1), last_ref[...])
        gap = ce_ref[pc_ref[slot]] - ve_ref[pv_ref[slot]]
        live = jnp.where(slot < count_ref[0], 1.0, 0.0)
        factor = live * jnp.sqrt(4.0 / jnp.full((1, LANES), gap, jnp.float32)) / np.float32(
            np.sqrt(np.float32(GRID**3)))
        amp[slot * LANES:slot * LANES + LANES, :] = (spectrum * factor).T.astype(jnp.bfloat16)

    per = CHUNK // LANES

    def pick(chunk, carry):
        cells = jnp.concatenate(
            [g_ref[pl.ds(chunk * per + at, 1), :] for at in range(per)], axis=1)
        lanes = pl.ds(pl.multiple_of(chunk * CHUNK, CHUNK), CHUNK)
        flat[0:4, lanes] = select(cells, amp[...])
        return carry

    lax.fori_loop(0, flat.shape[1] // CHUNK, pick, 0, unroll=3)
    for place in range(n_xy):
        starts = [(z * n_xy + place) * sub for z in range(3)]
        block = jnp.concatenate([flat[0:doubled, at:at + sub] for at in starts], axis=1)
        rows_ref[place] = block.astype(jnp.bfloat16)
    targets = flat.shape[1] // width
    for at in range(width // LANES):
        for target in range(targets):
            lane = target * width + at * LANES
            ordered[at, pl.ds(target, doubled, stride=targets), :] = flat[
                0:doubled, lane:lane + LANES]
        col_ref[0, :, at * LANES:(at + 1) * LANES] = ordered[at].astype(jnp.bfloat16)


def amplitudes_of(pv, pc, count, ve, ce, valence, conduction, g_index, n_xy, wide_sub, n_gcol):
    hbm = pl.BlockSpec(memory_space=pltpu.HBM)
    consts = [jnp.asarray(table) for table in tables()]
    g_rows = g_index.reshape(-1, LANES)
    arrays = [valence, conduction, *consts, g_rows]
    doubled = 2 * pv.shape[0]
    width = g_index.shape[0] // n_gcol
    return pl.pallas_call(
        amplitude_kernel,
        out_shape=(
            jax.ShapeDtypeStruct((1, doubled * n_gcol, width), jnp.bfloat16),
            jax.ShapeDtypeStruct((n_xy, doubled, wide_sub), jnp.bfloat16)),
        in_specs=[hbm] * 13,
        out_specs=(pl.BlockSpec(memory_space=pltpu.VMEM),) * 2,
        scratch_shapes=[pltpu.SMEM(a.shape, a.dtype) for a in (pv, pc, count, ve, ce)]
        + [pltpu.VMEM(a.shape, a.dtype) for a in arrays]
        + [
            pltpu.VMEM((4, 8 * ROWS, LANES), jnp.float32),
            pltpu.VMEM((ROWS, ROWS), jnp.bfloat16),
            pltpu.VMEM((8, g_index.shape[0]), jnp.float32),
            pltpu.VMEM((width // LANES, doubled * n_gcol, LANES), jnp.float32),
            pltpu.SemaphoreType.DMA((13,)),
        ],
        compiler_params=pltpu.CompilerParams(vmem_limit_bytes=60 * 1024 * 1024),
        cost_estimate=pl.CostEstimate(flops=4 * 10**9, bytes_accessed=5 * 10**6, transcendentals=0),
    )(pv, pc, count, ve, ce, *arrays)


def spread_kernel(in_ref, row_ref, out_ref, same_ref, wide):
    del row_ref, same_ref
    n_gcol, depth, width = in_ref.shape
    mine = position("gcol")
    for at in range(width // LANES):
        lanes = slice(at * LANES, (at + 1) * LANES)
        wide[at] = in_ref[:, :, lanes].astype(jnp.float32).reshape(n_gcol * depth, LANES)
        block = jnp.concatenate(
            [wide[at, pl.ds(row * n_gcol + mine, n_gcol, stride=depth), :]
             for row in range(depth // n_gcol)], axis=0).astype(jnp.bfloat16)
        for target in range(out_ref.shape[0]):
            out_ref[target, :, lanes] = block


def spread(col, row, copies):
    n_gcol, depth, width = col.shape
    vmem = pl.BlockSpec(memory_space=pltpu.VMEM)
    return pl.pallas_call(
        spread_kernel,
        out_shape=(jax.ShapeDtypeStruct((copies, depth, width), jnp.bfloat16),
                   jax.ShapeDtypeStruct(row.shape, row.dtype)),
        in_specs=[vmem, pl.BlockSpec(memory_space=pl.ANY)],
        out_specs=(vmem, pl.BlockSpec(memory_space=pl.ANY)),
        input_output_aliases={1: 1},
        scratch_shapes=[pltpu.VMEM((width // LANES, n_gcol * depth, LANES), jnp.float32)],
        compiler_params=pltpu.CompilerParams(vmem_limit_bytes=16 * 1024 * 1024),
        cost_estimate=pl.CostEstimate(flops=10**6, bytes_accessed=2 * 10**6, transcendentals=0),
    )(col, row)


def tile_kernel(row_ref, col_ref, own_ref, *refs):
    sent_refs, (wide, total) = refs[:-2], refs[-2:]
    n_xy, depth, width = col_ref.shape
    n_gcol, stride, wide_sub = row_ref.shape
    tiles = lane_tiles(wide_sub)
    for at, (lane, size) in enumerate(tiles):
        block = row_ref[:, :, lane:lane + size].astype(jnp.float32)
        wide[at, :, :size] = block.reshape(n_gcol * stride, size)
    value = None
    for source in range(NX):
        lefts = range(source * stride // NX, (source + 1) * stride // NX)
        left = jnp.concatenate(
            [jnp.concatenate([wide[at, pl.ds(place, n_gcol, stride=stride), :]
                              for place in lefts], axis=0)
             for at in range(len(tiles))], axis=1)[:, :wide_sub].astype(jnp.bfloat16)
        right = col_ref[source * n_xy // NX:(source + 1) * n_xy // NX]
        term = lax.dot_general(
            left, right.reshape(n_xy // NX * depth, width), (((0,), (0,)), ((), ())),
            preferred_element_type=jnp.float32)
        value = term if value is None else value + term
    total[...] = value
    sub = own_ref.shape[0]
    layer = position("pair") // NX
    own_ref[...] = total[pl.ds(pl.multiple_of(layer * sub, 8), sub), :]
    for at, sent_ref in enumerate(sent_refs):
        target = (layer + at + 1) % (len(sent_refs) + 1)
        sent_ref[...] = total[pl.ds(pl.multiple_of(target * sub, 8), sub), :].astype(jnp.bfloat16)


def tile(row, col, n_z):
    n_gcol, rows, wide_sub = row.shape
    width = col.shape[2]
    sub = wide_sub // n_z
    vmem = pl.BlockSpec(memory_space=pltpu.VMEM)
    return pl.pallas_call(
        tile_kernel,
        out_shape=[jax.ShapeDtypeStruct((sub, width), jnp.float32)]
        + [jax.ShapeDtypeStruct((sub, width), jnp.bfloat16)] * (n_z - 1),
        in_specs=[vmem] * 2,
        out_specs=[vmem] * n_z,
        scratch_shapes=[pltpu.VMEM((-(-wide_sub // LANES), n_gcol * rows, LANES), jnp.float32),
                        pltpu.VMEM((wide_sub, width), jnp.float32)],
        compiler_params=pltpu.CompilerParams(vmem_limit_bytes=40 * 1024 * 1024),
        cost_estimate=pl.CostEstimate(
            flops=2 * n_gcol * rows * wide_sub * width, bytes_accessed=5 * 10**6, transcendentals=0),
    )(row, col)


def local(valence, conduction, valence_energy, conduction_energy, pair_valence, pair_conduction,
          pair_count, g_index):
    n_pair, n_grow, n_gcol = (lax.axis_size(name) for name in ("pair", "grow", "gcol"))
    n_z = n_pair // NX
    total_g = g_index.shape[0]
    width = total_g // n_gcol
    sub = total_g // (n_pair * n_grow)
    n_xy = NX * n_grow
    xy_groups = [[(z * NX + x) * n_grow + y for x in range(NX) for y in range(n_grow)]
                 for z in range(n_z)]
    col, row = amplitudes_of(
        pair_valence, pair_conduction, pair_count, valence_energy, conduction_energy,
        valence, conduction, g_index, n_xy, n_z * sub, n_gcol)
    row = lax.all_to_all(row, ("pair", "grow"), 0, 0, tiled=True, axis_index_groups=xy_groups)
    col, row = spread(lax.all_gather(col, "gcol", axis=0, tiled=True), row, n_xy)
    col = lax.all_to_all(col, ("pair", "grow"), 0, 0, tiled=True, axis_index_groups=xy_groups)
    row = lax.all_gather(row.reshape(1, -1, n_z * sub), "gcol", axis=0, tiled=True)
    own, *sent = tile(row, col, n_z)
    for step, block in enumerate(sent, 1):
        own = own + lax.ppermute(block, "pair", [(z * NX + x, (z + step) % n_z * NX + x)
                                                 for z in range(n_z) for x in range(NX)])
    total_slots = pair_valence.shape[0] * n_pair * n_grow * n_gcol
    return -own / jnp.sqrt(jnp.float32(total_slots))


def solution(mesh):
    return jax.shard_map(
        local,
        mesh=mesh,
        in_specs=(
            P(),
            P("pair", None),
            P(),
            P("pair"),
            P(("pair", "grow", "gcol")),
            P(("pair", "grow", "gcol")),
            P(("pair", "grow", "gcol")),
            P(),
        ),
        out_specs=P(("pair", "grow"), "gcol"),
        check_vma=False,
    )
```

```python
import functools

import numpy as np
import ml_dtypes

import jax
import jax.numpy as jnp
from jax import lax
from jax.experimental import pallas as pl
from jax.experimental.pallas import tpu as pltpu
from jax.sharding import PartitionSpec as P

GRID = 32
NX = 4
LANES = 128
ROWS = 256
CHUNK = 768


def split(table):
    high = table.astype(ml_dtypes.bfloat16)
    low = (table - high.astype(np.float64)).astype(ml_dtypes.bfloat16)
    return high, low


def tables():
    turn = 2.0 * np.pi / GRID
    phase = turn * np.outer(np.arange(32), np.arange(16))
    first = np.concatenate(
        [np.kron(np.eye(4), np.cos(phase)), np.kron(np.eye(4), -np.sin(phase))], axis=1
    )
    high, low = split(first)
    both = np.concatenate([high, low], axis=1)
    lane_table = np.concatenate([both, both], axis=0)
    a_half = np.repeat(np.arange(16), 8)
    beta_half = np.tile(np.arange(8), 16)
    i_row = np.repeat(np.arange(32), 8)
    j_row = np.tile(np.arange(8), 32)
    phase = 2.0 * np.pi * (np.outer(a_half, i_row) / 32.0 + np.outer(beta_half, j_row) / 8.0)
    high, low = split(np.concatenate([np.cos(phase), np.sin(phase)], axis=0))
    row_table = np.concatenate([high, high, low], axis=1)
    beta = np.concatenate([beta_half, (8 - beta_half) % 8])
    angle = turn * np.outer(beta, np.repeat(np.arange(4), 16))
    twiddle_same = np.concatenate([np.cos(angle), np.cos(angle)], axis=1).astype(np.float32)
    twiddle_swap = np.concatenate([np.sin(angle), -np.sin(angle)], axis=1).astype(np.float32)
    step = np.outer(np.arange(4), np.arange(4)) % 4
    real = np.array([1, 0, -1, 0])[step]
    imag = np.array([0, -1, 0, 1])[step]
    last = np.block([[np.kron(real, np.eye(16)), np.kron(imag, np.eye(16))],
                     [np.kron(-imag, np.eye(16)), np.kron(real, np.eye(16))]])
    last_table = np.concatenate([last, last], axis=0).astype(ml_dtypes.bfloat16)
    return lane_table, row_table, twiddle_same, twiddle_swap, last_table


def halves(value):
    high = value.astype(jnp.bfloat16)
    low = (value - high.astype(jnp.float32)).astype(jnp.bfloat16)
    return high, low


def position(name):
    return lax.axis_index(name)


def dot(left, right):
    return jnp.dot(left, right, preferred_element_type=jnp.float32)


def select(cells, amplitudes):
    first = cells >> 10
    second = (cells >> 5) & 31
    third = cells & 31
    flip = third >= 16
    first = jnp.where(flip, (32 - first) & 31, first)
    second = jnp.where(flip, (32 - second) & 31, second)
    third = jnp.where(flip, 32 - third, third)
    sign = jnp.where(flip, -1.0, 1.0)
    beta = second & 7
    row = jnp.where(
        first > 16, 128 + (32 - first) * 8 + ((8 - beta) & 7), first * 8 + beta
    )
    lane = (second >> 3) * 16 + third
    width = cells.shape[-1]
    row_id = lax.broadcasted_iota(jnp.int32, (ROWS, width), 0).astype(jnp.bfloat16)
    one, zero = jnp.ones((), jnp.bfloat16), jnp.zeros((), jnp.bfloat16)
    hot = jnp.where(row_id == row.astype(jnp.bfloat16), one, zero)
    picked = dot(amplitudes, hot)
    mask = lax.broadcasted_iota(jnp.int32, (64, width), 0) == lane
    parts = []
    for part in range(4):
        block = jnp.where(mask, picked[part * 64:part * 64 + 64], 0.0)
        total = jnp.sum(block, axis=0, keepdims=True)
        parts.append(total * sign if part % 2 else total)
    return jnp.concatenate(parts, axis=0)


def lane_tiles(width):
    return [(lane, min(LANES, width - lane)) for lane in range(0, width, LANES)]


def amplitude_kernel(pv_hbm, pc_hbm, count_hbm, ve_hbm, ce_hbm, valence_hbm, conduction_hbm,
                     lane_hbm, row_hbm, same_hbm, swap_hbm, last_hbm, g_hbm,
                     col_ref, rows_ref, pv_ref, pc_ref, count_ref, ve_ref, ce_ref, valence_ref,
                     conduction_ref, lane_ref, row_ref, same_ref, swap_ref, last_ref, g_ref,
                     wide, amp, flat, ordered, sems):
    slots = 2
    n_xy, doubled, wide_sub = rows_ref.shape
    sub = wide_sub // 3
    width = col_ref.shape[2]
    sources = (pv_hbm, pc_hbm, conduction_hbm, valence_hbm, lane_hbm, row_hbm, same_hbm,
               swap_hbm, last_hbm, g_hbm, count_hbm, ve_hbm, ce_hbm)
    targets = (pv_ref, pc_ref, conduction_ref, valence_ref, lane_ref, row_ref, same_ref,
               swap_ref, last_ref, g_ref, count_ref, ve_ref, ce_ref)
    copies = [pltpu.make_async_copy(source, target, sems.at[at])
              for at, (source, target) in enumerate(zip(sources, targets))]
    for copy in copies:
        copy.start()
    for copy in copies[:3]:
        copy.wait()

    def widen(picks, tile, carry):
        lanes = pl.ds(pl.multiple_of(tile * LANES, LANES), LANES)
        rows = pl.ds(pl.multiple_of(tile * 8, 8), 8)
        for at, ref, band in picks:
            start = pl.multiple_of(band // 16 * 16, 16)
            block = ref[pl.ds(start, 16), lanes].astype(jnp.float32)
            wide[at, rows, :] = jnp.where(band % 16 >= 8, block[8:], block[:8])
        return carry

    picks = [(slots + slot, conduction_ref, pc_ref[slot]) for slot in range(slots)]
    lax.fori_loop(0, ROWS, functools.partial(widen, picks), 0, unroll=16)
    copies[3].wait()
    picks = [(slot, valence_ref, pv_ref[slot]) for slot in range(slots)]
    lax.fori_loop(0, ROWS, functools.partial(widen, picks), 0, unroll=16)
    for copy in copies[4:]:
        copy.wait()

    stage = []
    for slot in range(slots):
        left = wide[slot, pl.ds(pv_ref[slot] % 8, ROWS, stride=8), :]
        right = wide[slots + slot, pl.ds(pc_ref[slot] % 8, ROWS, stride=8), :]
        high, low = halves(left * right)
        out = dot(jnp.concatenate([high, low], axis=1), lane_ref[...])
        stage.append(out[:, :LANES] + out[:, LANES:])
    high, low = halves(jnp.concatenate(stage, axis=1))
    out = dot(row_ref[...], jnp.concatenate([high, low, high], axis=0))
    lane_id = lax.broadcasted_iota(jnp.int32, (LANES, LANES), 1)
    for slot in range(slots):
        lanes = slice(slot * LANES, slot * LANES + LANES)
        cosine, sine = out[:LANES, lanes], out[LANES:, lanes]
        turned = pltpu.roll(sine, 64, 1)
        turned = jnp.where(lane_id < 64, turned, -turned)
        full = jnp.concatenate([cosine + turned, cosine - turned], axis=0)
        full = full * same_ref[...] + pltpu.roll(full, 64, 1) * swap_ref[...]
        high, low = halves(full)
        spectrum = dot(jnp.concatenate([high, low], axis=1), last_ref[...])
        gap = ce_ref[pc_ref[slot]] - ve_ref[pv_ref[slot]]
        live = jnp.where(slot < count_ref[0], 1.0, 0.0)
        factor = live * jnp.sqrt(4.0 / jnp.full((1, LANES), gap, jnp.float32)) / np.float32(
            np.sqrt(np.float32(GRID**3)))
        amp[slot * LANES:slot * LANES + LANES, :] = (spectrum * factor).T.astype(jnp.bfloat16)

    per = CHUNK // LANES

    def pick(chunk, carry):
        cells = jnp.concatenate(
            [g_ref[pl.ds(chunk * per + at, 1), :] for at in range(per)], axis=1)
        lanes = pl.ds(pl.multiple_of(chunk * CHUNK, CHUNK), CHUNK)
        flat[0:4, lanes] = select(cells, amp[...])
        return carry

    lax.fori_loop(0, flat.shape[1] // CHUNK, pick, 0, unroll=4)
    for place in range(n_xy):
        starts = [(z * n_xy + place) * sub for z in range(3)]
        block = jnp.concatenate([flat[0:doubled, at:at + sub] for at in starts], axis=1)
        rows_ref[place] = block.astype(jnp.bfloat16)
    targets = flat.shape[1] // width
    for at in range(width // LANES):
        for target in range(targets):
            lane = target * width + at * LANES
            ordered[at, pl.ds(target, doubled, stride=targets), :] = flat[
                0:doubled, lane:lane + LANES]
        col_ref[0, :, at * LANES:(at + 1) * LANES] = ordered[at].astype(jnp.bfloat16)


def amplitudes_of(pv, pc, count, ve, ce, valence, conduction, g_index, n_xy, wide_sub, n_gcol):
    hbm = pl.BlockSpec(memory_space=pltpu.HBM)
    consts = [jnp.asarray(table) for table in tables()]
    g_rows = g_index.reshape(-1, LANES)
    arrays = [valence, conduction, *consts, g_rows]
    doubled = 2 * pv.shape[0]
    width = g_index.shape[0] // n_gcol
    return pl.pallas_call(
        amplitude_kernel,
        out_shape=(
            jax.ShapeDtypeStruct((1, doubled * n_gcol, width), jnp.bfloat16),
            jax.ShapeDtypeStruct((n_xy, doubled, wide_sub), jnp.bfloat16)),
        in_specs=[hbm] * 13,
        out_specs=(pl.BlockSpec(memory_space=pltpu.VMEM),) * 2,
        scratch_shapes=[pltpu.SMEM(a.shape, a.dtype) for a in (pv, pc, count, ve, ce)]
        + [pltpu.VMEM(a.shape, a.dtype) for a in arrays]
        + [
            pltpu.VMEM((4, 8 * ROWS, LANES), jnp.float32),
            pltpu.VMEM((ROWS, ROWS), jnp.bfloat16),
            pltpu.VMEM((8, g_index.shape[0]), jnp.float32),
            pltpu.VMEM((width // LANES, doubled * n_gcol, LANES), jnp.float32),
            pltpu.SemaphoreType.DMA((13,)),
        ],
        compiler_params=pltpu.CompilerParams(vmem_limit_bytes=60 * 1024 * 1024),
        cost_estimate=pl.CostEstimate(flops=4 * 10**9, bytes_accessed=5 * 10**6, transcendentals=0),
    )(pv, pc, count, ve, ce, *arrays)


def spread_kernel(in_ref, first_ref, out_ref, wide):
    del first_ref
    n_gcol, depth, width = in_ref.shape
    mine = position("gcol")
    for at in range(width // LANES):
        lanes = slice(at * LANES, (at + 1) * LANES)
        wide[at] = in_ref[:, :, lanes].astype(jnp.float32).reshape(n_gcol * depth, LANES)
        block = jnp.concatenate(
            [wide[at, pl.ds(row * n_gcol + mine, n_gcol, stride=depth), :]
             for row in range(depth // n_gcol)], axis=0).astype(jnp.bfloat16)
        for target in range(out_ref.shape[0]):
            out_ref[target, :, lanes] = block


def spread(col, first, n_grow):
    n_gcol, depth, width = col.shape
    vmem = pl.BlockSpec(memory_space=pltpu.VMEM)
    return pl.pallas_call(
        spread_kernel,
        out_shape=jax.ShapeDtypeStruct((n_grow, depth, width), jnp.bfloat16),
        in_specs=[vmem, pl.BlockSpec(memory_space=pl.ANY)],
        out_specs=vmem,
        scratch_shapes=[pltpu.VMEM((width // LANES, n_gcol * depth, LANES), jnp.float32)],
        compiler_params=pltpu.CompilerParams(vmem_limit_bytes=16 * 1024 * 1024),
        cost_estimate=pl.CostEstimate(flops=10**6, bytes_accessed=2 * 10**6, transcendentals=0),
    )(col, first)


def tile_kernel(row_ref, *refs):
    col_refs, own_ref, sent_refs = refs[:NX], refs[NX], refs[NX + 1:-2]
    wide, total = refs[-2:]
    n_grow, depth, width = col_refs[0].shape
    n_gcol, stride, wide_sub = row_ref.shape
    doubled = depth // n_gcol
    tiles = lane_tiles(wide_sub)
    for at, (lane, size) in enumerate(tiles):
        block = row_ref[:, :, lane:lane + size].astype(jnp.float32)
        wide[at, :, :size] = block.reshape(n_gcol * stride, size)
    mine = position("pair") % NX
    value = None
    for step, col_ref in enumerate(col_refs):
        first = (mine + (NX - step)) % NX * (n_grow * doubled)
        left = jnp.concatenate(
            [jnp.concatenate([wide[at, pl.ds(first + place, n_gcol, stride=stride), :]
                              for place in range(n_grow * doubled)], axis=0)
             for at in range(len(tiles))], axis=1)[:, :wide_sub].astype(jnp.bfloat16)
        term = lax.dot_general(
            left, col_ref[...].reshape(n_grow * depth, width), (((0,), (0,)), ((), ())),
            preferred_element_type=jnp.float32)
        value = term if value is None else value + term
    total[...] = value
    sub = own_ref.shape[0]
    layer = position("pair") // NX
    own_ref[...] = total[pl.ds(pl.multiple_of(layer * sub, 8), sub), :]
    for at, sent_ref in enumerate(sent_refs):
        target = (layer + at + 1) % (len(sent_refs) + 1)
        sent_ref[...] = total[pl.ds(pl.multiple_of(target * sub, 8), sub), :].astype(jnp.bfloat16)


def tile(row, cols, n_z):
    n_gcol, rows, wide_sub = row.shape
    width = cols[0].shape[2]
    sub = wide_sub // n_z
    vmem = pl.BlockSpec(memory_space=pltpu.VMEM)
    return pl.pallas_call(
        tile_kernel,
        out_shape=[jax.ShapeDtypeStruct((sub, width), jnp.float32)]
        + [jax.ShapeDtypeStruct((sub, width), jnp.bfloat16)] * (n_z - 1),
        in_specs=[vmem] * (1 + NX),
        out_specs=[vmem] * n_z,
        scratch_shapes=[pltpu.VMEM((-(-wide_sub // LANES), n_gcol * rows, LANES), jnp.float32),
                        pltpu.VMEM((wide_sub, width), jnp.float32)],
        compiler_params=pltpu.CompilerParams(vmem_limit_bytes=40 * 1024 * 1024),
        cost_estimate=pl.CostEstimate(
            flops=2 * n_gcol * rows * wide_sub * width, bytes_accessed=5 * 10**6, transcendentals=0),
    )(row, *cols)


def local(valence, conduction, valence_energy, conduction_energy, pair_valence, pair_conduction,
          pair_count, g_index):
    n_pair, n_grow, n_gcol = (lax.axis_size(name) for name in ("pair", "grow", "gcol"))
    n_z = n_pair // NX
    total_g = g_index.shape[0]
    width = total_g // n_gcol
    sub = total_g // (n_pair * n_grow)
    n_xy = NX * n_grow
    xy_groups = [[(z * NX + x) * n_grow + y for x in range(NX) for y in range(n_grow)]
                 for z in range(n_z)]
    col, row = amplitudes_of(
        pair_valence, pair_conduction, pair_count, valence_energy, conduction_energy,
        valence, conduction, g_index, n_xy, n_z * sub, n_gcol)
    row = lax.all_to_all(row, ("pair", "grow"), 0, 0, tiled=True, axis_index_groups=xy_groups)
    col = spread(lax.all_gather(col, "gcol", axis=0, tiled=True), row, n_grow)
    col = lax.all_to_all(col, "grow", 0, 0, tiled=True)
    row = lax.all_gather(row.reshape(1, -1, n_z * sub), "gcol", axis=0, tiled=True)
    cols = [col] + [
        lax.ppermute(col, "pair", [(z * NX + x, z * NX + (x + step) % NX)
                                   for z in range(n_z) for x in range(NX)])
        for step in range(1, NX)]
    own, *sent = tile(row, cols, n_z)
    for step, block in enumerate(sent, 1):
        own = own + lax.ppermute(block, "pair", [(z * NX + x, (z + step) % n_z * NX + x)
                                                 for z in range(n_z) for x in range(NX)])
    total_slots = pair_valence.shape[0] * n_pair * n_grow * n_gcol
    return -own / jnp.sqrt(jnp.float32(total_slots))


def solution(mesh):
    return jax.shard_map(
        local,
        mesh=mesh,
        in_specs=(
            P(),
            P("pair", None),
            P(),
            P("pair"),
            P(("pair", "grow", "gcol")),
            P(("pair", "grow", "gcol")),
            P(("pair", "grow", "gcol")),
            P(),
        ),
        out_specs=P(("pair", "grow"), "gcol"),
        check_vma=False,
    )
```

```python
import functools

import numpy as np
import ml_dtypes

import jax
import jax.numpy as jnp
from jax import lax
from jax.experimental import pallas as pl
from jax.experimental.pallas import tpu as pltpu
from jax.sharding import PartitionSpec as P

GRID = 32
NX = 4
LANES = 128
ROWS = 256
CHUNK = 768


def split(table):
    high = table.astype(ml_dtypes.bfloat16)
    low = (table - high.astype(np.float64)).astype(ml_dtypes.bfloat16)
    return high, low


def tables():
    turn = 2.0 * np.pi / GRID
    phase = turn * np.outer(np.arange(32), np.arange(16))
    first = np.concatenate(
        [np.kron(np.eye(4), np.cos(phase)), np.kron(np.eye(4), -np.sin(phase))], axis=1
    )
    high, low = split(first)
    both = np.concatenate([high, low], axis=1)
    lane_table = np.concatenate([both, both], axis=0)
    a_half = np.repeat(np.arange(16), 8)
    beta_half = np.tile(np.arange(8), 16)
    i_row = np.repeat(np.arange(32), 8)
    j_row = np.tile(np.arange(8), 32)
    phase = 2.0 * np.pi * (np.outer(a_half, i_row) / 32.0 + np.outer(beta_half, j_row) / 8.0)
    high, low = split(np.concatenate([np.cos(phase), np.sin(phase)], axis=0))
    row_table = np.concatenate([high, high, low], axis=1)
    beta = np.concatenate([beta_half, (8 - beta_half) % 8])
    angle = turn * np.outer(beta, np.repeat(np.arange(4), 16))
    twiddle_same = np.concatenate([np.cos(angle), np.cos(angle)], axis=1).astype(np.float32)
    twiddle_swap = np.concatenate([np.sin(angle), -np.sin(angle)], axis=1).astype(np.float32)
    step = np.outer(np.arange(4), np.arange(4)) % 4
    real = np.array([1, 0, -1, 0])[step]
    imag = np.array([0, -1, 0, 1])[step]
    last = np.block([[np.kron(real, np.eye(16)), np.kron(imag, np.eye(16))],
                     [np.kron(-imag, np.eye(16)), np.kron(real, np.eye(16))]])
    last_table = np.concatenate([last, last], axis=0).astype(ml_dtypes.bfloat16)
    return lane_table, row_table, twiddle_same, twiddle_swap, last_table


def halves(value):
    high = value.astype(jnp.bfloat16)
    low = (value - high.astype(jnp.float32)).astype(jnp.bfloat16)
    return high, low


def position(name):
    return lax.axis_index(name)


def dot(left, right):
    return jnp.dot(left, right, preferred_element_type=jnp.float32)


def select(cells, amplitudes):
    first = cells >> 10
    second = (cells >> 5) & 31
    third = cells & 31
    flip = third >= 16
    first = jnp.where(flip, (32 - first) & 31, first)
    second = jnp.where(flip, (32 - second) & 31, second)
    third = jnp.where(flip, 32 - third, third)
    sign = jnp.where(flip, -1.0, 1.0)
    beta = second & 7
    row = jnp.where(
        first > 16, 128 + (32 - first) * 8 + ((8 - beta) & 7), first * 8 + beta
    )
    lane = (second >> 3) * 16 + third
    width = cells.shape[-1]
    row_id = lax.broadcasted_iota(jnp.int32, (ROWS, width), 0).astype(jnp.bfloat16)
    one, zero = jnp.ones((), jnp.bfloat16), jnp.zeros((), jnp.bfloat16)
    hot = jnp.where(row_id == row.astype(jnp.bfloat16), one, zero)
    picked = dot(amplitudes, hot).astype(jnp.bfloat16)
    mask = lax.broadcasted_iota(jnp.int32, (64, width), 0).astype(jnp.bfloat16) == lane.astype(
        jnp.bfloat16)
    parts = []
    for part in range(4):
        block = jnp.where(mask, picked[part * 64:part * 64 + 64], zero)
        block = block[:32] + block[32:]
        block = (block[:16] + block[16:]).astype(jnp.float32)
        total = jnp.sum(block, axis=0, keepdims=True)
        parts.append(total * sign if part % 2 else total)
    return jnp.concatenate(parts, axis=0)


def lane_tiles(width):
    return [(lane, min(LANES, width - lane)) for lane in range(0, width, LANES)]


def amplitude_kernel(pv_hbm, pc_hbm, count_hbm, ve_hbm, ce_hbm, valence_hbm, conduction_hbm,
                     lane_hbm, row_hbm, same_hbm, swap_hbm, last_hbm, g_hbm,
                     col_ref, rows_ref, pv_ref, pc_ref, count_ref, ve_ref, ce_ref, valence_ref,
                     conduction_ref, lane_ref, row_ref, same_ref, swap_ref, last_ref, g_ref,
                     wide, amp, flat, placed, ordered, sems):
    slots = 2
    members, doubled, double_sub = rows_ref.shape
    wide_sub = double_sub // 2
    sub = wide_sub // 3
    n_xy = placed.shape[0]
    width = col_ref.shape[2]
    sources = (pv_hbm, pc_hbm, conduction_hbm, valence_hbm, lane_hbm, row_hbm, same_hbm,
               swap_hbm, last_hbm, g_hbm, count_hbm, ve_hbm, ce_hbm)
    targets = (pv_ref, pc_ref, conduction_ref, valence_ref, lane_ref, row_ref, same_ref,
               swap_ref, last_ref, g_ref, count_ref, ve_ref, ce_ref)
    copies = [pltpu.make_async_copy(source, target, sems.at[at])
              for at, (source, target) in enumerate(zip(sources, targets))]
    for copy in copies:
        copy.start()
    for copy in copies[:3]:
        copy.wait()

    def widen(picks, tile, carry):
        lanes = pl.ds(pl.multiple_of(tile * LANES, LANES), LANES)
        rows = pl.ds(pl.multiple_of(tile * 8, 8), 8)
        for at, ref, band in picks:
            start = pl.multiple_of(band // 16 * 16, 16)
            block = ref[pl.ds(start, 16), lanes].astype(jnp.float32)
            wide[at, rows, :] = jnp.where(band % 16 >= 8, block[8:], block[:8])
        return carry

    picks = [(slots + slot, conduction_ref, pc_ref[slot]) for slot in range(slots)]
    lax.fori_loop(0, ROWS, functools.partial(widen, picks), 0, unroll=16)
    copies[3].wait()
    picks = [(slot, valence_ref, pv_ref[slot]) for slot in range(slots)]
    lax.fori_loop(0, ROWS, functools.partial(widen, picks), 0, unroll=16)
    for copy in copies[4:]:
        copy.wait()

    stage = []
    for slot in range(slots):
        left = wide[slot, pl.ds(pv_ref[slot] % 8, ROWS, stride=8), :]
        right = wide[slots + slot, pl.ds(pc_ref[slot] % 8, ROWS, stride=8), :]
        high, low = halves(left * right)
        out = dot(jnp.concatenate([high, low], axis=1), lane_ref[...])
        stage.append(out[:, :LANES] + out[:, LANES:])
    high, low = halves(jnp.concatenate(stage, axis=1))
    out = dot(row_ref[...], jnp.concatenate([high, low, high], axis=0))
    lane_id = lax.broadcasted_iota(jnp.int32, (LANES, LANES), 1)
    for slot in range(slots):
        lanes = slice(slot * LANES, slot * LANES + LANES)
        cosine, sine = out[:LANES, lanes], out[LANES:, lanes]
        turned = pltpu.roll(sine, 64, 1)
        turned = jnp.where(lane_id < 64, turned, -turned)
        full = jnp.concatenate([cosine + turned, cosine - turned], axis=0)
        full = full * same_ref[...] + pltpu.roll(full, 64, 1) * swap_ref[...]
        high, low = halves(full)
        spectrum = dot(jnp.concatenate([high, low], axis=1), last_ref[...])
        gap = ce_ref[pc_ref[slot]] - ve_ref[pv_ref[slot]]
        live = jnp.where(slot < count_ref[0], 1.0, 0.0)
        factor = live * jnp.sqrt(4.0 / jnp.full((1, LANES), gap, jnp.float32)) / np.float32(
            np.sqrt(np.float32(GRID**3)))
        amp[slot * LANES:slot * LANES + LANES, :] = (spectrum * factor).T.astype(jnp.bfloat16)

    per = CHUNK // LANES

    def pick(chunk, carry):
        cells = jnp.concatenate(
            [g_ref[pl.ds(chunk * per + at, 1), :] for at in range(per)], axis=1)
        lanes = pl.ds(pl.multiple_of(chunk * CHUNK, CHUNK), CHUNK)
        flat[0:4, lanes] = select(cells, amp[...])
        return carry

    lax.fori_loop(0, flat.shape[1] // CHUNK, pick, 0, unroll=4)
    for place in range(n_xy):
        starts = [(z * n_xy + place) * sub for z in range(3)]
        block = jnp.concatenate([flat[0:doubled, at:at + sub] for at in starts], axis=1)
        placed[place, 0:doubled, 0:wide_sub] = block
    n_grow = members // 2
    low = position("pair") % NX // 2 * 2
    for member in range(members):
        own = low + member // n_grow
        near = placed[own * n_grow + member % n_grow]
        far = placed[(NX - 1 - own) * n_grow + member % n_grow]
        rows_ref[member] = jnp.concatenate(
            [near[0:doubled, 0:wide_sub], far[0:doubled, 0:wide_sub]], axis=1).astype(jnp.bfloat16)
    targets = flat.shape[1] // width
    for at in range(width // LANES):
        for target in range(targets):
            lane = target * width + at * LANES
            ordered[at, pl.ds(target, doubled, stride=targets), :] = flat[
                0:doubled, lane:lane + LANES]
        col_ref[0, :, at * LANES:(at + 1) * LANES] = ordered[at].astype(jnp.bfloat16)


def amplitudes_of(pv, pc, count, ve, ce, valence, conduction, g_index, n_xy, wide_sub, n_gcol):
    hbm = pl.BlockSpec(memory_space=pltpu.HBM)
    consts = [jnp.asarray(table) for table in tables()]
    g_rows = g_index.reshape(-1, LANES)
    arrays = [valence, conduction, *consts, g_rows]
    doubled = 2 * pv.shape[0]
    width = g_index.shape[0] // n_gcol
    return pl.pallas_call(
        amplitude_kernel,
        out_shape=(
            jax.ShapeDtypeStruct((1, doubled * n_gcol, width), jnp.bfloat16),
            jax.ShapeDtypeStruct((n_xy * 2 // NX, doubled, 2 * wide_sub), jnp.bfloat16)),
        in_specs=[hbm] * 13,
        out_specs=(pl.BlockSpec(memory_space=pltpu.VMEM),) * 2,
        scratch_shapes=[pltpu.SMEM(a.shape, a.dtype) for a in (pv, pc, count, ve, ce)]
        + [pltpu.VMEM(a.shape, a.dtype) for a in arrays]
        + [
            pltpu.VMEM((4, 8 * ROWS, LANES), jnp.float32),
            pltpu.VMEM((ROWS, ROWS), jnp.bfloat16),
            pltpu.VMEM((8, g_index.shape[0]), jnp.float32),
            pltpu.VMEM((n_xy, 8, wide_sub), jnp.float32),
            pltpu.VMEM((width // LANES, doubled * n_gcol, LANES), jnp.float32),
            pltpu.SemaphoreType.DMA((13,)),
        ],
        compiler_params=pltpu.CompilerParams(vmem_limit_bytes=60 * 1024 * 1024),
        cost_estimate=pl.CostEstimate(flops=4 * 10**9, bytes_accessed=5 * 10**6, transcendentals=0),
    )(pv, pc, count, ve, ce, *arrays)


def spread_kernel(in_ref, first_ref, out_ref, wide):
    del first_ref
    n_gcol, depth, width = in_ref.shape
    mine = position("gcol")
    for at in range(width // LANES):
        lanes = slice(at * LANES, (at + 1) * LANES)
        wide[at] = in_ref[:, :, lanes].astype(jnp.float32).reshape(n_gcol * depth, LANES)
        block = jnp.concatenate(
            [wide[at, pl.ds(row * n_gcol + mine, n_gcol, stride=depth), :]
             for row in range(depth // n_gcol)], axis=0).astype(jnp.bfloat16)
        for target in range(out_ref.shape[0]):
            out_ref[target, :, lanes] = block


def spread(col, first, n_grow):
    n_gcol, depth, width = col.shape
    vmem = pl.BlockSpec(memory_space=pltpu.VMEM)
    return pl.pallas_call(
        spread_kernel,
        out_shape=jax.ShapeDtypeStruct((n_grow, depth, width), jnp.bfloat16),
        in_specs=[vmem, pl.BlockSpec(memory_space=pl.ANY)],
        out_specs=vmem,
        scratch_shapes=[pltpu.VMEM((width // LANES, n_gcol * depth, LANES), jnp.float32)],
        compiler_params=pltpu.CompilerParams(vmem_limit_bytes=16 * 1024 * 1024),
        cost_estimate=pl.CostEstimate(flops=10**6, bytes_accessed=2 * 10**6, transcendentals=0),
    )(col, first)


def tile_kernel(row_ref, *refs):
    col_refs, own_ref, sent_refs = refs[:2], refs[2], refs[3:-2]
    wide, total = refs[-2:]
    n_grow, depth, width = col_refs[0].shape
    n_gcol, stride, double_sub = row_ref.shape
    tiles = lane_tiles(double_sub)
    for at, (lane, size) in enumerate(tiles):
        block = row_ref[:, :, lane:lane + size].astype(jnp.float32)
        wide[at, :, :size] = block.reshape(n_gcol * stride, size)
    mine = position("pair") % 2
    value = None
    for step, col_ref in enumerate(col_refs):
        first = (mine + step) % 2 * (stride // 2)
        left = jnp.concatenate(
            [jnp.concatenate([wide[at, pl.ds(first + place, n_gcol, stride=stride), :]
                              for place in range(stride // 2)], axis=0)
             for at in range(len(tiles))], axis=1)[:, :double_sub].astype(jnp.bfloat16)
        term = lax.dot_general(
            left, col_ref[...].reshape(n_grow * depth, width), (((0,), (0,)), ((), ())),
            preferred_element_type=jnp.float32)
        value = term if value is None else value + term
    total[...] = value
    sub = own_ref.shape[0]
    layers = double_sub // (2 * sub)
    layer = position("pair") // NX
    for at, out_ref in enumerate((own_ref, *sent_refs)):
        row = at // layers * layers + (layer + at) % layers
        block = total[pl.ds(pl.multiple_of(row * sub, 8), sub), :]
        out_ref[...] = block.astype(out_ref.dtype)


def tile(row, cols, n_z):
    n_gcol, rows, double_sub = row.shape
    width = cols[0].shape[2]
    sub = double_sub // (2 * n_z)
    vmem = pl.BlockSpec(memory_space=pltpu.VMEM)
    return pl.pallas_call(
        tile_kernel,
        out_shape=[jax.ShapeDtypeStruct((sub, width), jnp.float32)]
        + [jax.ShapeDtypeStruct((sub, width), jnp.bfloat16)] * (2 * n_z - 1),
        in_specs=[vmem] * 3,
        out_specs=[vmem] * (2 * n_z),
        scratch_shapes=[pltpu.VMEM((-(-double_sub // LANES), n_gcol * rows, LANES), jnp.float32),
                        pltpu.VMEM((double_sub, width), jnp.float32)],
        compiler_params=pltpu.CompilerParams(vmem_limit_bytes=40 * 1024 * 1024),
        cost_estimate=pl.CostEstimate(
            flops=2 * n_gcol * rows * double_sub * width, bytes_accessed=5 * 10**6,
            transcendentals=0),
    )(row, *cols)


def local(valence, conduction, valence_energy, conduction_energy, pair_valence, pair_conduction,
          pair_count, g_index):
    n_pair, n_grow, n_gcol = (lax.axis_size(name) for name in ("pair", "grow", "gcol"))
    n_z = n_pair // NX
    total_g = g_index.shape[0]
    width = total_g // n_gcol
    sub = total_g // (n_pair * n_grow)
    n_xy = NX * n_grow
    near_groups = [[(z * NX + 2 * half + x) * n_grow + y for x in range(2) for y in range(n_grow)]
                   for z in range(n_z) for half in range(NX // 2)]
    col, row = amplitudes_of(
        pair_valence, pair_conduction, pair_count, valence_energy, conduction_energy,
        valence, conduction, g_index, n_xy, n_z * sub, n_gcol)
    row = lax.all_to_all(row, ("pair", "grow"), 0, 0, tiled=True, axis_index_groups=near_groups)
    col = spread(lax.all_gather(col, "gcol", axis=0, tiled=True), row, n_grow)
    col = lax.all_to_all(col, "grow", 0, 0, tiled=True)
    row = lax.all_gather(row.reshape(1, -1, 2 * n_z * sub), "gcol", axis=0, tiled=True)
    devices = [(z, x) for z in range(n_z) for x in range(NX)]
    beside = lax.ppermute(col, "pair", [(z * NX + x, z * NX + (x ^ 1)) for z, x in devices])
    own, *sent = tile(row, [col, beside], n_z)
    for at, block in enumerate(sent, 1):
        own = own + lax.ppermute(block, "pair", [
            (z * NX + x, (z + at) % n_z * NX + (NX - 1 - x if at >= n_z else x))
            for z, x in devices])
    total_slots = pair_valence.shape[0] * n_pair * n_grow * n_gcol
    return -own / jnp.sqrt(jnp.float32(total_slots))


def solution(mesh):
    return jax.shard_map(
        local,
        mesh=mesh,
        in_specs=(
            P(),
            P("pair", None),
            P(),
            P("pair"),
            P(("pair", "grow", "gcol")),
            P(("pair", "grow", "gcol")),
            P(("pair", "grow", "gcol")),
            P(),
        ),
        out_specs=P(("pair", "grow"), "gcol"),
        check_vma=False,
    )
```

```python
import functools

import numpy as np
import ml_dtypes

import jax
import jax.numpy as jnp
from jax import lax
from jax.experimental import pallas as pl
from jax.experimental.pallas import tpu as pltpu
from jax.sharding import PartitionSpec as P

GRID = 32
NX = 4
LANES = 128
ROWS = 256
CHUNK = 768


def split(table):
    high = table.astype(ml_dtypes.bfloat16)
    low = (table - high.astype(np.float64)).astype(ml_dtypes.bfloat16)
    return high, low


def tables():
    turn = 2.0 * np.pi / GRID
    phase = turn * np.outer(np.arange(32), np.arange(16))
    first = np.concatenate(
        [np.kron(np.eye(4), np.cos(phase)), np.kron(np.eye(4), -np.sin(phase))], axis=1
    )
    high, low = split(first)
    both = np.concatenate([high, low], axis=1)
    lane_table = np.concatenate([both, both], axis=0)
    a_half = np.repeat(np.arange(16), 8)
    beta_half = np.tile(np.arange(8), 16)
    i_row = np.repeat(np.arange(32), 8)
    j_row = np.tile(np.arange(8), 32)
    phase = 2.0 * np.pi * (np.outer(a_half, i_row) / 32.0 + np.outer(beta_half, j_row) / 8.0)
    high, low = split(np.concatenate([np.cos(phase), np.sin(phase)], axis=0))
    row_table = np.concatenate([high, high, low], axis=1)
    beta = np.concatenate([beta_half, (8 - beta_half) % 8])
    angle = turn * np.outer(beta, np.repeat(np.arange(4), 16))
    twiddle_same = np.concatenate([np.cos(angle), np.cos(angle)], axis=1).astype(np.float32)
    twiddle_swap = np.concatenate([np.sin(angle), -np.sin(angle)], axis=1).astype(np.float32)
    step = np.outer(np.arange(4), np.arange(4)) % 4
    real = np.array([1, 0, -1, 0])[step]
    imag = np.array([0, -1, 0, 1])[step]
    last = np.block([[np.kron(real, np.eye(16)), np.kron(imag, np.eye(16))],
                     [np.kron(-imag, np.eye(16)), np.kron(real, np.eye(16))]])
    last_table = np.concatenate([last, last], axis=0).astype(ml_dtypes.bfloat16)
    return lane_table, row_table, twiddle_same, twiddle_swap, last_table


def halves(value):
    high = value.astype(jnp.bfloat16)
    low = (value - high.astype(jnp.float32)).astype(jnp.bfloat16)
    return high, low


def position(name):
    return lax.axis_index(name)


def dot(left, right):
    return jnp.dot(left, right, preferred_element_type=jnp.float32)


def select(cells, amplitudes):
    first = cells >> 10
    second = (cells >> 5) & 31
    third = cells & 31
    flip = third >= 16
    first = jnp.where(flip, (32 - first) & 31, first)
    second = jnp.where(flip, (32 - second) & 31, second)
    third = jnp.where(flip, 32 - third, third)
    sign = jnp.where(flip, -1.0, 1.0)
    beta = second & 7
    row = jnp.where(
        first > 16, 128 + (32 - first) * 8 + ((8 - beta) & 7), first * 8 + beta
    )
    lane = (second >> 3) * 16 + third
    width = cells.shape[-1]
    row_id = lax.broadcasted_iota(jnp.int32, (ROWS, width), 0).astype(jnp.bfloat16)
    one, zero = jnp.ones((), jnp.bfloat16), jnp.zeros((), jnp.bfloat16)
    hot = jnp.where(row_id == row.astype(jnp.bfloat16), one, zero)
    picked = dot(amplitudes, hot).astype(jnp.bfloat16)
    mask = lax.broadcasted_iota(jnp.int32, (64, width), 0).astype(jnp.bfloat16) == lane.astype(
        jnp.bfloat16)
    parts = []
    for part in range(4):
        block = jnp.where(mask, picked[part * 64:part * 64 + 64], zero)
        block = block[:32] + block[32:]
        block = (block[:16] + block[16:]).astype(jnp.float32)
        total = jnp.sum(block, axis=0, keepdims=True)
        parts.append(total * sign if part % 2 else total)
    return jnp.concatenate(parts, axis=0)


def lane_tiles(width):
    return [(lane, min(LANES, width - lane)) for lane in range(0, width, LANES)]


def amplitude_kernel(pv_hbm, pc_hbm, count_hbm, ve_hbm, ce_hbm, valence_hbm, conduction_hbm,
                     lane_hbm, row_hbm, same_hbm, swap_hbm, last_hbm, g_hbm,
                     col_ref, rows_ref, pv_ref, pc_ref, count_ref, ve_ref, ce_ref, valence_ref,
                     conduction_ref, lane_ref, row_ref, same_ref, swap_ref, last_ref, g_ref,
                     wide, amp, flat, placed, ordered, sems):
    slots = 2
    members, doubled, double_sub = rows_ref.shape
    wide_sub = double_sub // 2
    sub = wide_sub // 3
    n_xy = placed.shape[0]
    width = col_ref.shape[2]
    sources = (pv_hbm, pc_hbm, conduction_hbm, valence_hbm, lane_hbm, row_hbm, same_hbm,
               swap_hbm, last_hbm, g_hbm, count_hbm, ve_hbm, ce_hbm)
    targets = (pv_ref, pc_ref, conduction_ref, valence_ref, lane_ref, row_ref, same_ref,
               swap_ref, last_ref, g_ref, count_ref, ve_ref, ce_ref)
    copies = [pltpu.make_async_copy(source, target, sems.at[at])
              for at, (source, target) in enumerate(zip(sources, targets))]
    for copy in copies:
        copy.start()
    for copy in copies[:3]:
        copy.wait()

    def widen(picks, tile, carry):
        lanes = pl.ds(pl.multiple_of(tile * LANES, LANES), LANES)
        rows = pl.ds(pl.multiple_of(tile * 8, 8), 8)
        for at, ref, band in picks:
            start = pl.multiple_of(band // 16 * 16, 16)
            block = ref[pl.ds(start, 16), lanes].astype(jnp.float32)
            wide[at, rows, :] = jnp.where(band % 16 >= 8, block[8:], block[:8])
        return carry

    picks = [(slots + slot, conduction_ref, pc_ref[slot]) for slot in range(slots)]
    lax.fori_loop(0, ROWS, functools.partial(widen, picks), 0, unroll=16)
    copies[3].wait()
    picks = [(slot, valence_ref, pv_ref[slot]) for slot in range(slots)]
    lax.fori_loop(0, ROWS, functools.partial(widen, picks), 0, unroll=16)
    for copy in copies[4:]:
        copy.wait()

    stage = []
    for slot in range(slots):
        left = wide[slot, pl.ds(pv_ref[slot] % 8, ROWS, stride=8), :]
        right = wide[slots + slot, pl.ds(pc_ref[slot] % 8, ROWS, stride=8), :]
        high, low = halves(left * right)
        out = dot(jnp.concatenate([high, low], axis=1), lane_ref[...])
        stage.append(out[:, :LANES] + out[:, LANES:])
    high, low = halves(jnp.concatenate(stage, axis=1))
    out = dot(row_ref[...], jnp.concatenate([high, low, high], axis=0))
    lane_id = lax.broadcasted_iota(jnp.int32, (LANES, LANES), 1)
    for slot in range(slots):
        lanes = slice(slot * LANES, slot * LANES + LANES)
        cosine, sine = out[:LANES, lanes], out[LANES:, lanes]
        turned = pltpu.roll(sine, 64, 1)
        turned = jnp.where(lane_id < 64, turned, -turned)
        full = jnp.concatenate([cosine + turned, cosine - turned], axis=0)
        full = full * same_ref[...] + pltpu.roll(full, 64, 1) * swap_ref[...]
        high, low = halves(full)
        spectrum = dot(jnp.concatenate([high, low], axis=1), last_ref[...])
        gap = ce_ref[pc_ref[slot]] - ve_ref[pv_ref[slot]]
        live = jnp.where(slot < count_ref[0], 1.0, 0.0)
        factor = live * jnp.sqrt(4.0 / jnp.full((1, LANES), gap, jnp.float32)) / np.float32(
            np.sqrt(np.float32(GRID**3)))
        amp[slot * LANES:slot * LANES + LANES, :] = (spectrum * factor).T.astype(jnp.bfloat16)

    per = CHUNK // LANES

    def pick(chunk, carry):
        cells = jnp.concatenate(
            [g_ref[pl.ds(chunk * per + at, 1), :] for at in range(per)], axis=1)
        lanes = pl.ds(pl.multiple_of(chunk * CHUNK, CHUNK), CHUNK)
        flat[0:4, lanes] = select(cells, amp[...])
        return carry

    lax.fori_loop(0, flat.shape[1] // CHUNK, pick, 0, unroll=4)
    for place in range(n_xy):
        starts = [(z * n_xy + place) * sub for z in range(3)]
        block = jnp.concatenate([flat[0:doubled, at:at + sub] for at in starts], axis=1)
        placed[place, 0:doubled, 0:wide_sub] = block
    parity = position("grow") % 2
    for member in range(members):
        near = placed[2 * member + parity]
        far = placed[2 * member + 1 - parity]
        rows_ref[member] = jnp.concatenate(
            [near[0:doubled, 0:wide_sub], far[0:doubled, 0:wide_sub]], axis=1).astype(jnp.bfloat16)
    targets = flat.shape[1] // width
    for at in range(width // LANES):
        for target in range(targets):
            lane = target * width + at * LANES
            ordered[at, pl.ds(target, doubled, stride=targets), :] = flat[
                0:doubled, lane:lane + LANES]
        col_ref[0, :, at * LANES:(at + 1) * LANES] = ordered[at].astype(jnp.bfloat16)


def amplitudes_of(pv, pc, count, ve, ce, valence, conduction, g_index, n_xy, wide_sub, n_gcol):
    hbm = pl.BlockSpec(memory_space=pltpu.HBM)
    consts = [jnp.asarray(table) for table in tables()]
    g_rows = g_index.reshape(-1, LANES)
    arrays = [valence, conduction, *consts, g_rows]
    doubled = 2 * pv.shape[0]
    width = g_index.shape[0] // n_gcol
    return pl.pallas_call(
        amplitude_kernel,
        out_shape=(
            jax.ShapeDtypeStruct((1, doubled * n_gcol, width), jnp.bfloat16),
            jax.ShapeDtypeStruct((n_xy // 2, doubled, 2 * wide_sub), jnp.bfloat16)),
        in_specs=[hbm] * 13,
        out_specs=(pl.BlockSpec(memory_space=pltpu.VMEM),) * 2,
        scratch_shapes=[pltpu.SMEM(a.shape, a.dtype) for a in (pv, pc, count, ve, ce)]
        + [pltpu.VMEM(a.shape, a.dtype) for a in arrays]
        + [
            pltpu.VMEM((4, 8 * ROWS, LANES), jnp.float32),
            pltpu.VMEM((ROWS, ROWS), jnp.bfloat16),
            pltpu.VMEM((8, g_index.shape[0]), jnp.float32),
            pltpu.VMEM((n_xy, 8, wide_sub), jnp.float32),
            pltpu.VMEM((width // LANES, doubled * n_gcol, LANES), jnp.float32),
            pltpu.SemaphoreType.DMA((13,)),
        ],
        compiler_params=pltpu.CompilerParams(vmem_limit_bytes=60 * 1024 * 1024),
        cost_estimate=pl.CostEstimate(flops=4 * 10**9, bytes_accessed=5 * 10**6, transcendentals=0),
    )(pv, pc, count, ve, ce, *arrays)


def spread_kernel(in_ref, first_ref, out_ref, wide):
    del first_ref
    n_gcol, depth, width = in_ref.shape
    mine = position("gcol")
    for at in range(width // LANES):
        lanes = slice(at * LANES, (at + 1) * LANES)
        wide[at] = in_ref[:, :, lanes].astype(jnp.float32).reshape(n_gcol * depth, LANES)
        block = jnp.concatenate(
            [wide[at, pl.ds(row * n_gcol + mine, n_gcol, stride=depth), :]
             for row in range(depth // n_gcol)], axis=0).astype(jnp.bfloat16)
        for target in range(out_ref.shape[0]):
            out_ref[target, :, lanes] = block


def spread(col, first, n_grow):
    n_gcol, depth, width = col.shape
    vmem = pl.BlockSpec(memory_space=pltpu.VMEM)
    return pl.pallas_call(
        spread_kernel,
        out_shape=jax.ShapeDtypeStruct((n_grow, depth, width), jnp.bfloat16),
        in_specs=[vmem, pl.BlockSpec(memory_space=pl.ANY)],
        out_specs=vmem,
        scratch_shapes=[pltpu.VMEM((width // LANES, n_gcol * depth, LANES), jnp.float32)],
        compiler_params=pltpu.CompilerParams(vmem_limit_bytes=16 * 1024 * 1024),
        cost_estimate=pl.CostEstimate(flops=10**6, bytes_accessed=2 * 10**6, transcendentals=0),
    )(col, first)


def tile_kernel(row_ref, *refs):
    col_refs, own_ref, sent_refs = refs[:NX], refs[NX], refs[NX + 1:-2]
    wide, total = refs[-2:]
    n_half, depth, width = col_refs[0].shape
    n_gcol, stride, double_sub = row_ref.shape
    tiles = lane_tiles(double_sub)
    for at, (lane, size) in enumerate(tiles):
        block = row_ref[:, :, lane:lane + size].astype(jnp.float32)
        wide[at, :, :size] = block.reshape(n_gcol * stride, size)
    mine = position("pair") % NX
    value = None
    for step, col_ref in enumerate(col_refs):
        first = (mine + (NX - step)) % NX * (stride // NX)
        left = jnp.concatenate(
            [jnp.concatenate([wide[at, pl.ds(first + place, n_gcol, stride=stride), :]
                              for place in range(stride // NX)], axis=0)
             for at in range(len(tiles))], axis=1)[:, :double_sub].astype(jnp.bfloat16)
        term = lax.dot_general(
            left, col_ref[...].reshape(n_half * depth, width), (((0,), (0,)), ((), ())),
            preferred_element_type=jnp.float32)
        value = term if value is None else value + term
    total[...] = value
    sub = own_ref.shape[0]
    layers = double_sub // (2 * sub)
    layer = position("pair") // NX
    for at, out_ref in enumerate((own_ref, *sent_refs)):
        row = at // layers * layers + (layer + at) % layers
        block = total[pl.ds(pl.multiple_of(row * sub, 8), sub), :]
        out_ref[...] = block.astype(out_ref.dtype)


def tile(row, cols, n_z):
    n_gcol, rows, double_sub = row.shape
    width = cols[0].shape[2]
    sub = double_sub // (2 * n_z)
    vmem = pl.BlockSpec(memory_space=pltpu.VMEM)
    return pl.pallas_call(
        tile_kernel,
        out_shape=[jax.ShapeDtypeStruct((sub, width), jnp.float32)]
        + [jax.ShapeDtypeStruct((sub, width), jnp.bfloat16)] * (2 * n_z - 1),
        in_specs=[vmem] * (1 + NX),
        out_specs=[vmem] * (2 * n_z),
        scratch_shapes=[pltpu.VMEM((-(-double_sub // LANES), n_gcol * rows, LANES), jnp.float32),
                        pltpu.VMEM((double_sub, width), jnp.float32)],
        compiler_params=pltpu.CompilerParams(vmem_limit_bytes=40 * 1024 * 1024),
        cost_estimate=pl.CostEstimate(
            flops=2 * n_gcol * rows * double_sub * width, bytes_accessed=5 * 10**6,
            transcendentals=0),
    )(row, *cols)


def local(valence, conduction, valence_energy, conduction_energy, pair_valence, pair_conduction,
          pair_count, g_index):
    n_pair, n_grow, n_gcol = (lax.axis_size(name) for name in ("pair", "grow", "gcol"))
    n_z = n_pair // NX
    total_g = g_index.shape[0]
    width = total_g // n_gcol
    sub = total_g // (n_pair * n_grow)
    n_xy = NX * n_grow
    halves_y = [list(range(parity, n_grow, 2)) for parity in range(2)]
    near_groups = [[(z * NX + x) * n_grow + y for x in range(NX) for y in half]
                   for z in range(n_z) for half in halves_y]
    col, row = amplitudes_of(
        pair_valence, pair_conduction, pair_count, valence_energy, conduction_energy,
        valence, conduction, g_index, n_xy, n_z * sub, n_gcol)
    row = lax.all_to_all(row, ("pair", "grow"), 0, 0, tiled=True, axis_index_groups=near_groups)
    col = spread(lax.all_gather(col, "gcol", axis=0, tiled=True), row, n_grow // 2)
    col = lax.all_to_all(col, "grow", 0, 0, tiled=True, axis_index_groups=halves_y)
    row = lax.all_gather(row.reshape(1, -1, 2 * n_z * sub), "gcol", axis=0, tiled=True)
    cols = [col] + [
        lax.ppermute(col, "pair", [(z * NX + x, z * NX + (x + step) % NX)
                                   for z in range(n_z) for x in range(NX)])
        for step in range(1, NX)]
    own, *sent = tile(row, cols, n_z)
    for at, block in enumerate(sent, 1):
        own = own + lax.ppermute(block, ("pair", "grow"), [
            ((z * NX + x) * n_grow + y,
             ((z + at) % n_z * NX + x) * n_grow + (y ^ 1 if at >= n_z else y))
            for z in range(n_z) for x in range(NX) for y in range(n_grow)])
    total_slots = pair_valence.shape[0] * n_pair * n_grow * n_gcol
    return -own / jnp.sqrt(jnp.float32(total_slots))


def solution(mesh):
    return jax.shard_map(
        local,
        mesh=mesh,
        in_specs=(
            P(),
            P("pair", None),
            P(),
            P("pair"),
            P(("pair", "grow", "gcol")),
            P(("pair", "grow", "gcol")),
            P(("pair", "grow", "gcol")),
            P(),
        ),
        out_specs=P(("pair", "grow"), "gcol"),
        check_vma=False,
    )
```
